32 devices in a mesh: wide: 8 (over z, x), narrow: 4 (over y, core).
Axes of the slice: x: 2, y: 2, z: 4, core: 2. Of those that a mesh axis runs over, the one named last changes fastest.
Arguments:
- amps: bfloat16 [64, 128, 128], P(('wide', 'narrow')), may hold values from -4 to 4
- resp: bfloat16 [64, 128, 128], P(('wide', 'narrow')), may hold values from -4 to 4
- trans: bfloat16 [64, 512, 128], P(('wide', 'narrow')), may hold values from -0.375 to 0.375
- ints: bfloat16 [64, 128, 128], P(('wide', 'narrow')), may hold values from -6 to 6
- energies: float32 [64, 128], P(('wide', 'narrow')), may hold values from 0.5 to 4
- couple: float32 [64, 12], P(('wide', 'narrow')), may hold values from -1 to 1
- readers: int32 [64, 12], P(('wide', 'narrow')), may hold values from 0 to 15, as said below
- domains: int32 [64, 4], replicated, may hold values from 0 to 7, as said below
- integrals: bfloat16 [1024, 512], P(None, 'narrow'), may hold values from -0.01171875 to 0.01171875
Outputs:
- new_amps: float32 [64, 128, 128], P(('wide', 'narrow'))
- new_resp: float32 [64, 128, 128], P(('wide', 'narrow'))
- response: float32 [1024, 512], P('wide', 'narrow')
The draws below stay inside these ranges and needn't reach their ends.
Inputs may be any that keep to these rules, and one draw needn't show every extreme that they name: `readers`: each row lists 12 different positions among the 16 pairs of the same narrow index. `domains`: each row lists 4 different function blocks.
All inputs are finite; a program needn't handle non-finite values.
Results may differ from the reference program's by a relative error of at most 0.015.
Values may be sent and summed in bfloat16 or wider, within the bound.
No kernel may reach another device: no remote copies, remote signals or barrier semaphores. Data moves between devices by JAX's collectives and lax.ppermute only.
A program may use at most 64 MiB of HBM per device.

```python
import math
import jax
import jax.numpy as jnp
from jax import lax

NPNO = 128
NFUN = 512
BLK = 128
NFB = 8
NCOL = 512
PAIRS_DEV = 2
DOM_BLK = 4
NBAS = 1024
ROW_PAIRS = 16
READERS = 12
PAIRS = 64
N_WIDE = 8
N_NARROW = 4


def draw_readers(key, part):
    scores = jax.random.randint(key, (PAIRS, ROW_PAIRS), 0, 1 << 20) * ROW_PAIRS + jnp.arange(ROW_PAIRS, dtype=jnp.int32)[None, :]
    order = jnp.argsort(scores, axis=1, stable=True)
    return order[:, :READERS].astype(jnp.int32)


def draw_domains(key, part):
    scores = jax.random.randint(key, (PAIRS, NFB), 0, 1 << 20) * NFB + jnp.arange(NFB, dtype=jnp.int32)[None, :]
    order = jnp.argsort(scores, axis=1, stable=True)
    return order[:, :DOM_BLK].astype(jnp.int32)


def level_of(key, shape, cuts, low, top_value):
    level = 1.0
    for dim, parts in cuts:
        draws = jax.random.uniform(jax.random.fold_in(jax.random.fold_in(key, 6), dim), (parts,), jnp.float32, low / len(cuts), top_value / len(cuts))
        level = level * jnp.repeat(jnp.exp(draws), shape[dim] // parts).reshape((-1,) + (1,) * (len(shape) - 1 - dim))
    return level


def scatter_about(key, extent, scale, most, split=(), kind=jnp.bfloat16):
    entries = jax.random.normal(key, extent, jnp.float32) * scale
    if len(split) > 0:
        entries = level_of(key, extent, split, -0.22, 0.18) * entries
    return jnp.clip(entries, min=-most, max=most).astype(kind)


def setup_inputs(seed: int = 0) -> dict:
    keys = jax.random.split(jax.random.key(seed), 10)
    amps = scatter_about(keys[0], (PAIRS, NPNO, NPNO), 0.5, 4.0, ((0, 32),))
    resp = scatter_about(keys[1], (PAIRS, NPNO, NPNO), 0.5, 4.0, ((0, 32),))
    trans = scatter_about(keys[2], (PAIRS, NFUN, NPNO), (NFUN // 2) ** -0.5, 0.375, ((0, 32),))
    ints = scatter_about(keys[3], (PAIRS, NPNO, NPNO), 1.0, 6.0, ((0, 32),))
    energies = jnp.clip(jnp.exp(math.log(4.0) - 2.0794415 * jax.random.uniform(keys[4], (PAIRS, NPNO), jnp.float32) ** level_of(keys[4], (PAIRS, NPNO), ((0, 32),), -0.2, 0.2)), 0.5, 4.0)
    couple = scatter_about(keys[5], (PAIRS, READERS), 0.2, 1.0, ((0, 32),), jnp.float32)
    readers = draw_readers(jax.random.fold_in(keys[9], 71), 0)
    domains = draw_domains(jax.random.fold_in(keys[9], 71), 0)
    integrals = scatter_about(keys[8], (NBAS, NCOL), (256 * NBAS) ** -0.5, 0.01171875, ((1, 4),))
    return dict(amps=amps, resp=resp, trans=trans, ints=ints, energies=energies, couple=couple, readers=readers, domains=domains, integrals=integrals)


def to_rows(values):
    rest = values.shape[1:]
    grouped = values.reshape((N_WIDE, N_NARROW, PAIRS_DEV) + rest)
    return jnp.swapaxes(grouped, 0, 1).reshape((N_NARROW, N_WIDE * PAIRS_DEV) + rest)


def reader_terms(own_q, own_dom, their_q, their_dom, their_amps):
    blocks = own_q.shape[0]
    reader_count = their_q.shape[0]
    matches = (own_dom[None, :, None] == their_dom[:, None, :]).astype(jnp.float32)
    split_q = their_q.reshape(reader_count, blocks, BLK, NPNO).astype(jnp.float32)
    shifted = jnp.einsum('sab,sbfp->safp', matches, split_q).astype(jnp.bfloat16)
    intersection = jnp.einsum('afp,safq->spq', own_q.astype(jnp.float32), shifted.astype(jnp.float32)).astype(jnp.bfloat16)
    halfway = jnp.einsum('spq,sqc->spc', intersection.astype(jnp.float32), their_amps.astype(jnp.float32)).astype(jnp.bfloat16)
    halfway = halfway.reshape(reader_count, NPNO, 2, NPNO)
    return jnp.einsum('spkc,sqc->skpq', halfway.astype(jnp.float32), intersection.astype(jnp.float32))


def reference(amps, resp, trans, ints, energies, couple, readers, domains, integrals):
    dom_blk = NFUN // BLK
    pair_amps = jnp.concatenate([amps, resp], axis=2)
    q_rows = to_rows(trans)
    amp_rows = to_rows(pair_amps)
    dom_rows = to_rows(domains)

    def one_pair(position):
        row_index = (position // PAIRS_DEV) % N_NARROW
        picks = readers[position]
        contrib = reader_terms(trans[position].reshape(dom_blk, BLK, NPNO), domains[position],
                               q_rows[row_index, picks], dom_rows[row_index, picks], amp_rows[row_index, picks])
        return jnp.einsum('s,skpq->kpq', couple[position], contrib)

    coupled = lax.map(one_pair, jnp.arange(PAIRS, dtype=jnp.int32))
    amps_f = amps.astype(jnp.float32)
    resp_f = resp.astype(jnp.float32)
    denominator = energies[:, :, None] + energies[:, None, :]
    new_amps = amps_f - 0.5 * (ints.astype(jnp.float32) + denominator * amps_f + coupled[:, 0]) / denominator
    new_resp = resp_f - 0.5 * (amps_f + denominator * resp_f + coupled[:, 1]) / denominator
    amps_b = new_amps.astype(jnp.bfloat16).astype(jnp.float32)
    resp_b = new_resp.astype(jnp.bfloat16).astype(jnp.float32)
    weights = 0.5 * (jnp.einsum('gpc,gqc->gpq', amps_b, resp_b) + jnp.einsum('gpc,gqc->gpq', resp_b, amps_b))
    weights = weights.astype(jnp.bfloat16)
    block_ids = jnp.arange(NFB, dtype=jnp.int32)

    def density_step(total, items):
        q_one, dom_one, w_one = items
        place = (block_ids[:, None] == dom_one[None, :]).astype(jnp.float32)
        full_q = jnp.einsum('nd,dfp->nfp', place, q_one.reshape(dom_blk, BLK, NPNO).astype(jnp.float32))
        full_q = full_q.reshape(NBAS, NPNO).astype(jnp.bfloat16)
        left = jnp.dot(full_q, w_one, preferred_element_type=jnp.float32).astype(jnp.bfloat16)
        return total + jnp.dot(left, full_q.T, preferred_element_type=jnp.float32), None

    density, _ = lax.scan(density_step, jnp.zeros((NBAS, NBAS), jnp.float32), (trans, domains, weights))
    response = jnp.dot(density, integrals.astype(jnp.float32), precision=lax.Precision.HIGHEST)
    return new_amps, new_resp, response
```

```python
import functools

import jax
import jax.numpy as jnp
from jax import lax
from jax.experimental import pallas as pl
from jax.experimental.pallas import tpu as pltpu
from jax.sharding import PartitionSpec as P

BF16 = jnp.bfloat16
F32 = jnp.float32
SMEM = pl.BlockSpec(memory_space=pltpu.SMEM)
VMEM = pl.BlockSpec(memory_space=pltpu.VMEM)


def swap(value, axis, mask):
    size = lax.axis_size(axis)
    return lax.ppermute(value, axis, [(i, i ^ mask) for i in range(size)])


def call(kernel, out_shape, specs, *args):
    return pl.pallas_call(
        kernel,
        out_shape=out_shape,
        in_specs=specs,
        out_specs=jax.tree.map(lambda _: VMEM, out_shape),
        compiler_params=pltpu.CompilerParams(vmem_limit_bytes=32 * 1024 * 1024),
    )(*args)


def amps_kernel(amps_ref, resp_ref, out_ref):
    npno = amps_ref.shape[1]
    for p in range(amps_ref.shape[0]):
        out_ref[p, :, :npno] = amps_ref[p]
        out_ref[p, :, npno:] = resp_ref[p]


def spread_kernel(blk, narrow, mask, where_ref, dom_ref, own_ref, far_ref, out_ref):
    pairs, _, npno = own_ref.shape
    dom_blk = own_ref.shape[1] // blk
    out_ref[...] = jnp.zeros_like(out_ref)
    for side, q_ref in enumerate((own_ref, far_ref)):
        dev = where_ref[0] ^ (mask * side)
        for p in range(pairs):
            pair = (dev * narrow + where_ref[1]) * pairs + p
            for a in range(dom_blk):
                rows = pl.ds((side * pairs + p) * npno, npno)
                out_ref[dom_ref[pair * dom_blk + a], rows, :] = q_ref[p, a * blk : (a + 1) * blk, :].T


def couple_kernel(masks, blk, narrow, last, *refs):
    count = len(masks)
    where_ref, dom_ref, own_c_ref, far_c_ref, spread_ref = refs[:5]
    q_refs, tz_refs = refs[5 : 5 + count], refs[5 + count : 5 + 2 * count]
    rest = refs[5 + 2 * count :]
    pairs, _, npno = q_refs[0].shape
    dom_blk = q_refs[0].shape[1] // blk
    sums = [None] * (2 * pairs)
    if last:
        sums = [rest[0][g] for g in range(2 * pairs)]
    for k, mask in enumerate(masks):
        dev = where_ref[0] ^ mask
        overlap, half = [], []
        for p in range(pairs):
            pair = (dev * narrow + where_ref[1]) * pairs + p
            left = jnp.concatenate([spread_ref[dom_ref[pair * dom_blk + b]] for b in range(dom_blk)], axis=1)
            s = jnp.dot(left, q_refs[k][p], preferred_element_type=F32).astype(BF16)
            h = jnp.dot(s, tz_refs[k][p], preferred_element_type=F32)
            scaled = []
            for g in range(2 * pairs):
                c_ref = own_c_ref if g < pairs else far_c_ref
                c = c_ref[g % pairs, dev * pairs + p]
                scaled.append((h[g * npno : (g + 1) * npno] * c).astype(BF16))
            overlap.append(s)
            half.append(scaled)
        for g in range(2 * pairs):
            rows = slice(g * npno, (g + 1) * npno)
            right = jnp.concatenate([s[rows] for s in overlap], axis=1)
            left = jnp.concatenate(
                [jnp.concatenate([h[g][:, i * npno : (i + 1) * npno] for h in half], axis=1) for i in range(2)], axis=0
            )
            term = lax.dot_general(left, right, (((1,), (1,)), ((), ())), preferred_element_type=F32)
            sums[g] = term if sums[g] is None else sums[g] + term
    if last:
        own_ref, far_ref = rest[1:]
        for g in range(pairs):
            own_ref[g] = sums[g]
            far_ref[g] = sums[pairs + g].astype(BF16)
    else:
        for g in range(2 * pairs):
            rest[0][g] = sums[g]


def update_kernel(own_ref, back_ref, amps_ref, resp_ref, ints_ref, energy_ref, new_amps_ref, new_resp_ref, w_ref):
    npno = amps_ref.shape[1]
    for p in range(amps_ref.shape[0]):
        across = jnp.broadcast_to(energy_ref[pl.ds(p, 1), :], (npno, npno))
        denom = across + across.T
        amps = amps_ref[p].astype(F32)
        resp = resp_ref[p].astype(F32)
        coupled_t = own_ref[p, :npno] + back_ref[p, :npno].astype(F32)
        coupled_z = own_ref[p, npno:] + back_ref[p, npno:].astype(F32)
        new_amps = amps - 0.5 * (ints_ref[p].astype(F32) + denom * amps + coupled_t) / denom
        new_resp = resp - 0.5 * (amps + denom * resp + coupled_z) / denom
        new_amps_ref[p] = new_amps
        new_resp_ref[p] = new_resp
        prod = lax.dot_general(
            new_amps.astype(BF16), new_resp.astype(BF16), (((1,), (1,)), ((), ())), preferred_element_type=F32
        )
        w_ref[p] = (0.5 * (prod + prod.T)).astype(BF16)


def place_kernel(blk, narrow, *refs):
    where_ref, dom_ref, ints_ref = refs[:3]
    q_refs, (full_ref, moved_ref) = refs[3 : 3 + narrow], refs[3 + narrow :]
    pairs, _, npno = q_refs[0].shape
    dom_blk = q_refs[0].shape[1] // blk
    full_ref[...] = jnp.zeros_like(full_ref)
    for k in range(narrow):
        for p in range(pairs):
            pair = (where_ref[0] * narrow + (where_ref[1] ^ k)) * pairs + p
            slot = k * pairs + p
            blocks = []
            for a in range(dom_blk):
                f = dom_ref[pair * dom_blk + a]
                full_ref[f, :, slot * npno : (slot + 1) * npno] = q_refs[k][p, a * blk : (a + 1) * blk, :]
                blocks.append(ints_ref[f])
            moved_ref[slot] = lax.dot_general(
                q_refs[k][p], jnp.concatenate(blocks, axis=0), (((0,), (0,)), ((), ())), preferred_element_type=F32
            ).astype(BF16)


def response_kernel(*refs):
    full_ref, moved_ref = refs[:2]
    w_refs, out_ref = refs[2:-1], refs[-1]
    pairs = w_refs[0].shape[0]
    parts = []
    for k, w_ref in enumerate(w_refs):
        for p in range(pairs):
            parts.append(jnp.dot(w_ref[p], moved_ref[k * pairs + p], preferred_element_type=F32).astype(BF16))
    right = jnp.concatenate(parts, axis=0)
    blocks, blk, depth = full_ref.shape
    rows = jnp.dot(full_ref[...].reshape(blocks * blk, depth), right, preferred_element_type=F32).astype(BF16)
    out_ref[...] = rows.reshape(out_ref.shape)


def per_device(amps, resp, trans, ints, energies, couple, readers, domains, integrals):
    wide, narrow = lax.axis_size("wide"), lax.axis_size("narrow")
    pairs, nfun, npno = trans.shape
    blk = nfun // domains.shape[1]
    nbas, cols = integrals.shape
    near = wide // 2
    partner = wide - 2
    sds = jax.ShapeDtypeStruct

    where = jnp.stack([lax.axis_index("wide"), lax.axis_index("narrow")]).astype(jnp.int32)
    dom = domains.reshape(-1)
    position = jnp.arange(wide * pairs, dtype=jnp.int32)
    own_c = jnp.sum(jnp.where(readers[:, :, None] == position, couple[:, :, None], 0.0), axis=1)

    amps_resp = call(amps_kernel, sds((pairs, npno, 2 * npno), BF16), [VMEM, VMEM], amps, resp)
    near_q, near_tz = {0: trans}, {0: amps_resp}
    near_q[1] = swap(trans, "wide", 1)
    for mask in range(2, near, 2):
        near_q[mask] = swap(trans, "wide", mask)
    near_tz[1] = swap(amps_resp, "wide", 1)
    for mask in range(2, near, 2):
        near_tz[mask] = swap(amps_resp, "wide", mask)
    far_q = swap(trans, "wide", partner)
    far_c = swap(own_c, "wide", partner)
    for mask in range(2, near, 2):
        near_q[mask + 1] = swap(near_q[mask], "wide", 1)
        near_tz[mask + 1] = swap(near_tz[mask], "wide", 1)
    narrow_q = {0: trans}
    for mask in range(1, narrow):
        narrow_q[mask] = swap(narrow_q[mask - 1], "narrow", 1) if mask % 2 else swap(trans, "narrow", mask)

    spread = call(
        functools.partial(spread_kernel, blk, narrow, partner),
        sds((nbas // blk, 2 * pairs * npno, blk), BF16),
        [SMEM, SMEM, VMEM, VMEM],
        where, dom, trans, far_q,
    )
    full, moved = call(
        functools.partial(place_kernel, blk, narrow),
        (sds((nbas // blk, blk, narrow * pairs * npno), BF16), sds((narrow * pairs, npno, cols), BF16)),
        [SMEM, SMEM] + [VMEM] * (1 + narrow),
        where, dom, integrals.reshape(nbas // blk, blk, cols), *[narrow_q[k] for k in range(narrow)],
    )
    early = [0, 1] + list(range(2, near, 2))
    late = list(range(3, near, 2))
    sums = call(
        functools.partial(couple_kernel, early, blk, narrow, False),
        sds((2 * pairs, 2 * npno, npno), F32),
        [SMEM] * 4 + [VMEM] * (1 + 2 * len(early)),
        where, dom, own_c, far_c, spread, *[near_q[m] for m in early], *[near_tz[m] for m in early],
    )
    own, far = call(
        functools.partial(couple_kernel, late, blk, narrow, True),
        (sds((pairs, 2 * npno, npno), F32), sds((pairs, 2 * npno, npno), BF16)),
        [SMEM] * 4 + [VMEM] * (2 + 2 * len(late)),
        where, dom, own_c, far_c, spread, *[near_q[m] for m in late], *[near_tz[m] for m in late], sums,
    )
    back = swap(far, "wide", partner)
    mats = sds((pairs, npno, npno), F32)
    new_amps, new_resp, weights = call(
        update_kernel,
        (mats, mats, sds((pairs, npno, npno), BF16)),
        [VMEM] * 6,
        own, back, amps, resp, ints, energies,
    )
    narrow_w = {0: weights}
    for mask in range(1, narrow):
        narrow_w[mask] = swap(narrow_w[mask - 1], "narrow", 1) if mask % 2 else swap(weights, "narrow", mask)
    partial = call(
        response_kernel,
        sds((wide, nbas // wide, cols), BF16),
        [VMEM] * (2 + narrow),
        full, moved, *[narrow_w[k] for k in range(narrow)],
    )
    shares = lax.all_to_all(partial, "wide", 0, 0, tiled=True)
    response = jnp.sum(shares.astype(F32), axis=0)
    return (new_amps, new_resp, response)


def solution(mesh):
    in_specs = (
        P(("wide", "narrow"), None, None),
        P(("wide", "narrow"), None, None),
        P(("wide", "narrow"), None, None),
        P(("wide", "narrow"), None, None),
        P(("wide", "narrow"), None),
        P(("wide", "narrow"), None),
        P(("wide", "narrow"), None),
        P(),
        P(None, "narrow"),
    )
    out_specs = (
        P(("wide", "narrow"), None, None),
        P(("wide", "narrow"), None, None),
        P("wide", "narrow"),
    )
    return jax.shard_map(
        per_device, mesh=mesh, in_specs=in_specs, out_specs=out_specs, check_vma=False
    )
```

```python
import functools

import jax
import jax.numpy as jnp
from jax import lax
from jax.experimental import pallas as pl
from jax.experimental.pallas import tpu as pltpu
from jax.sharding import PartitionSpec as P

BF16 = jnp.bfloat16
F32 = jnp.float32
SMEM = pl.BlockSpec(memory_space=pltpu.SMEM)
VMEM = pl.BlockSpec(memory_space=pltpu.VMEM)
ANY = pl.BlockSpec(memory_space=pl.ANY)


def swap(value, axis, mask):
    size = lax.axis_size(axis)
    return lax.ppermute(value, axis, [(i, i ^ mask) for i in range(size)])


def call(kernel, out_shape, specs, micros, *args, scratch=()):
    return pl.pallas_call(
        kernel,
        out_shape=out_shape,
        in_specs=specs,
        out_specs=jax.tree.map(lambda _: VMEM, out_shape),
        scratch_shapes=scratch,
        cost_estimate=pl.CostEstimate(flops=int(micros * 1e9), bytes_accessed=0, transcendentals=0),
        compiler_params=pltpu.CompilerParams(vmem_limit_bytes=32 * 1024 * 1024),
    )(*args)


def join_kernel(amps_ref, resp_ref, out_ref, sems):
    npno = amps_ref.shape[1]
    copies = []
    for i, ref in enumerate((amps_ref, resp_ref)):
        copy = pltpu.make_async_copy(ref, out_ref.at[:, :, pl.ds(i * npno, npno)], sems.at[i])
        copy.start()
        copies.append(copy)
    for copy in copies:
        copy.wait()


def pack_kernel(blk, readers_ref, couple_ref, q_ref, after_ref, out_ref):
    del after_ref
    pairs, nfun, npno = q_ref.shape
    count = (out_ref.shape[1] - nfun) // 2
    row = lax.broadcasted_iota(jnp.int32, (count, npno), 0)
    for p in range(pairs):
        for a in range(nfun // blk):
            rows = slice(a * blk, (a + 1) * blk)
            out_ref[p, rows, :] = q_ref[p, rows, :].T
        c = jnp.zeros((count, npno), F32)
        for r in range(readers_ref.shape[1]):
            c = c + jnp.where(row == readers_ref[p, r], couple_ref[p, r], 0.0)
        high = c.astype(BF16)
        out_ref[p, nfun : nfun + count, :] = high
        out_ref[p, nfun + count :, :] = (c - high.astype(F32)).astype(BF16)


def load_coefficients(pack_ref, c_ref):
    count = c_ref.shape[1]
    nfun = pack_ref.shape[1] - 2 * count
    for p in range(pack_ref.shape[0]):
        c_ref[p] = pack_ref[p, nfun : nfun + count, :].astype(F32) + pack_ref[p, nfun + count :, :].astype(F32)


def add_terms(sums, overlaps, tz_ref, c_ref, dev):
    pairs, npno, _ = tz_ref.shape
    half = []
    for p, s in enumerate(overlaps):
        h = jnp.dot(s, tz_ref[p], preferred_element_type=F32)
        scaled = []
        for g in range(pairs):
            c = c_ref[g, pl.ds(dev * pairs + p, 1), :]
            c = jnp.concatenate([c, c], axis=1)
            scaled.append((h[g * npno : (g + 1) * npno] * c).astype(BF16))
        half.append(scaled)
    for g in range(pairs):
        rows = slice(g * npno, (g + 1) * npno)
        right = jnp.concatenate([s[rows] for s in overlaps], axis=1)
        left = jnp.concatenate(
            [jnp.concatenate([h[g][:, i * npno : (i + 1) * npno] for h in half], axis=1) for i in range(2)], axis=0
        )
        term = lax.dot_general(left, right, (((1,), (1,)), ((), ())), preferred_element_type=F32)
        sums[g] = term if sums[g] is None else sums[g] + term


def couple_kernel(masks, ahead, blk, narrow, flip, prior, *refs):
    where_ref, dom_ref, pack_ref = refs[:3]
    refs = refs[3:]
    q_refs, refs = refs[: len(masks) + len(ahead)], refs[len(masks) + len(ahead) :]
    tz_refs, refs = refs[: len(masks)], refs[len(masks) :]
    prior_ref, refs = (refs[0], refs[1:]) if prior else (None, refs)
    out_ref, spread_ref, c_ref = refs[0], refs[-2], refs[-1]
    pairs, _, npno = q_refs[0].shape
    dom_blk = q_refs[0].shape[1] // blk
    load_coefficients(pack_ref, c_ref)
    spread_ref[...] = jnp.zeros_like(spread_ref)
    for p in range(pairs):
        pair = ((where_ref[0] ^ flip) * narrow + where_ref[1]) * pairs + p
        for a in range(dom_blk):
            spread_ref[dom_ref[pair * dom_blk + a], p * npno : (p + 1) * npno, :] = pack_ref[
                p, a * blk : (a + 1) * blk, :
            ]
    sums = [prior_ref[g] if prior else None for g in range(pairs)]
    for k, mask in enumerate(masks + ahead):
        dev = where_ref[0] ^ mask
        overlaps = []
        for p in range(pairs):
            pair = (dev * narrow + where_ref[1]) * pairs + p
            left = jnp.concatenate([spread_ref[dom_ref[pair * dom_blk + b]] for b in range(dom_blk)], axis=1)
            overlaps.append(jnp.dot(left, q_refs[k][p], preferred_element_type=F32).astype(BF16))
        if k < len(masks):
            add_terms(sums, overlaps, tz_refs[k], c_ref, dev)
        else:
            for p in range(pairs):
                refs[1][(k - len(masks)) * pairs + p] = overlaps[p]
    for g in range(pairs):
        out_ref[g] = sums[g].astype(out_ref.dtype)


def finish_kernel(masks, *refs):
    where_ref, pack_ref, overlap_ref, prior_ref = refs[:4]
    tz_refs, (out_ref, c_ref) = refs[4 : 4 + len(masks)], refs[4 + len(masks) :]
    pairs = pack_ref.shape[0]
    load_coefficients(pack_ref, c_ref)
    sums = [prior_ref[g] for g in range(pairs)]
    for k, mask in enumerate(masks):
        overlaps = [overlap_ref[k * pairs + p] for p in range(pairs)]
        add_terms(sums, overlaps, tz_refs[k], c_ref, where_ref[0] ^ mask)
    for g in range(pairs):
        out_ref[g] = sums[g].astype(out_ref.dtype)


def update_kernel(own_ref, back_ref, amps_ref, resp_ref, ints_ref, energy_ref, new_amps_ref, new_resp_ref, w_ref):
    npno = amps_ref.shape[1]
    for p in range(amps_ref.shape[0]):
        across = jnp.broadcast_to(energy_ref[pl.ds(p, 1), :], (npno, npno))
        denom = across + across.T
        amps = amps_ref[p].astype(F32)
        resp = resp_ref[p].astype(F32)
        coupled_t = own_ref[p, :npno] + back_ref[p, :npno].astype(F32)
        coupled_z = own_ref[p, npno:] + back_ref[p, npno:].astype(F32)
        new_amps = amps - 0.5 * (ints_ref[p].astype(F32) + denom * amps + coupled_t) / denom
        new_resp = resp - 0.5 * (amps + denom * resp + coupled_z) / denom
        new_amps_ref[p] = new_amps
        new_resp_ref[p] = new_resp
        prod = lax.dot_general(
            new_amps.astype(BF16), new_resp.astype(BF16), (((1,), (1,)), ((), ())), preferred_element_type=F32
        )
        w_ref[p] = (0.5 * (prod + prod.T)).astype(BF16)


def place_kernel(blk, narrow, *refs):
    where_ref, dom_ref, ints_ref = refs[:3]
    q_refs, (full_ref, moved_ref) = refs[3 : 3 + narrow], refs[3 + narrow :]
    pairs, _, npno = q_refs[0].shape
    dom_blk = q_refs[0].shape[1] // blk
    full_ref[...] = jnp.zeros_like(full_ref)
    for k in range(narrow):
        for p in range(pairs):
            pair = (where_ref[0] * narrow + (where_ref[1] ^ k)) * pairs + p
            slot = k * pairs + p
            blocks = []
            for a in range(dom_blk):
                f = dom_ref[pair * dom_blk + a]
                full_ref[f, :, slot * npno : (slot + 1) * npno] = q_refs[k][p, a * blk : (a + 1) * blk, :]
                blocks.append(ints_ref[f])
            moved_ref[slot] = lax.dot_general(
                q_refs[k][p], jnp.concatenate(blocks, axis=0), (((0,), (0,)), ((), ())), preferred_element_type=F32
            ).astype(BF16)


def response_kernel(*refs):
    full_ref, moved_ref = refs[:2]
    w_refs, out_ref = refs[2:-1], refs[-1]
    pairs = w_refs[0].shape[0]
    parts = []
    for k, w_ref in enumerate(w_refs):
        for p in range(pairs):
            parts.append(jnp.dot(w_ref[p], moved_ref[k * pairs + p], preferred_element_type=F32).astype(BF16))
    right = jnp.concatenate(parts, axis=0)
    blocks, blk, depth = full_ref.shape
    rows = jnp.dot(full_ref[...].reshape(blocks * blk, depth), right, preferred_element_type=F32).astype(BF16)
    out_ref[...] = rows.reshape(out_ref.shape)


def per_device(amps, resp, trans, ints, energies, couple, readers, domains, integrals):
    wide, narrow = lax.axis_size("wide"), lax.axis_size("narrow")
    pairs, nfun, npno = trans.shape
    blk = nfun // domains.shape[1]
    nbas, cols = integrals.shape
    near = wide // 2
    partner = wide - 2
    sds = jax.ShapeDtypeStruct

    count = wide * pairs
    where = jnp.stack([lax.axis_index("wide"), lax.axis_index("narrow")]).astype(jnp.int32)
    dom = domains.reshape(-1)

    near_q, near_tz = {0: trans}, {}
    near_q[1] = swap(trans, "wide", 1)
    for mask in range(2, near, 2):
        near_q[mask] = swap(trans, "wide", mask)
    near_tz[0] = call(
        join_kernel, sds((pairs, npno, 2 * npno), BF16), [ANY, ANY], 1, amps, resp, scratch=[pltpu.SemaphoreType.DMA((2,))]
    )
    near_tz[1] = swap(near_tz[0], "wide", 1)
    for mask in range(2, near, 2):
        near_tz[mask] = swap(near_tz[0], "wide", mask)
    pack = call(
        functools.partial(pack_kernel, blk),
        sds((pairs, nfun + 2 * count, npno), BF16),
        [SMEM, SMEM, VMEM, ANY], 1,
        readers, couple, trans, near_q[near - 2],
    )
    far_pack = swap(pack, "wide", partner)
    for mask in range(2, near, 2):
        near_q[mask + 1] = swap(near_q[mask], "wide", 1)
        near_tz[mask + 1] = swap(near_tz[mask], "wide", 1)
    narrow_q = {0: trans}
    for mask in range(1, narrow):
        narrow_q[mask] = swap(narrow_q[mask - 1], "narrow", 1) if mask % 2 else swap(trans, "narrow", mask)

    full, moved = call(
        functools.partial(place_kernel, blk, narrow),
        (sds((nbas // blk, blk, narrow * pairs * npno), BF16), sds((narrow * pairs, npno, cols), BF16)),
        [SMEM, SMEM] + [VMEM] * (1 + narrow), 2,
        where, dom, integrals.reshape(nbas // blk, blk, cols), *[narrow_q[k] for k in range(narrow)],
    )
    early = [0, 1] + list(range(2, near, 2))
    late = list(range(3, near, 2))
    scratch = [
        pltpu.VMEM((nbas // blk, pairs * npno, blk), BF16),
        pltpu.VMEM((pairs, count, npno), F32),
    ]
    sums = sds((pairs, 2 * npno, npno), F32)
    own = call(
        functools.partial(couple_kernel, early, [], blk, narrow, 0, False),
        sums,
        [SMEM] * 2 + [VMEM] * (1 + 2 * len(early)), 2,
        where, dom, pack, *[near_q[m] for m in early], *[near_tz[m] for m in early],
        scratch=scratch,
    )
    far, overlap = call(
        functools.partial(couple_kernel, early, late, blk, narrow, partner, False),
        (sums, sds((len(late) * pairs, pairs * npno, npno), BF16)),
        [SMEM] * 2 + [VMEM] * (1 + 2 * len(early) + len(late)), 3,
        where, dom, far_pack, *[near_q[m] for m in early + late], *[near_tz[m] for m in early],
        scratch=scratch,
    )
    far = call(
        functools.partial(finish_kernel, late),
        sds(sums.shape, BF16),
        [SMEM] + [VMEM] * (3 + len(late)), 1,
        where, far_pack, overlap, far, *[near_tz[m] for m in late],
        scratch=scratch[1:],
    )
    back = swap(far, "wide", partner)
    own = call(
        functools.partial(couple_kernel, late, [], blk, narrow, 0, True),
        sums,
        [SMEM] * 2 + [VMEM] * (2 + 2 * len(late)), 2,
        where, dom, pack, *[near_q[m] for m in late], *[near_tz[m] for m in late], own,
        scratch=scratch,
    )
    mats = sds((pairs, npno, npno), F32)
    new_amps, new_resp, weights = call(
        update_kernel,
        (mats, mats, sds((pairs, npno, npno), BF16)),
        [VMEM] * 6, 1,
        own, back, amps, resp, ints, energies,
    )
    narrow_w = {0: weights}
    for mask in range(1, narrow):
        narrow_w[mask] = swap(narrow_w[mask - 1], "narrow", 1) if mask % 2 else swap(weights, "narrow", mask)
    partial = call(
        response_kernel,
        sds((wide, nbas // wide, cols), BF16),
        [VMEM] * (2 + narrow), 1,
        full, moved, *[narrow_w[k] for k in range(narrow)],
    )
    shares = lax.all_to_all(partial, "wide", 0, 0, tiled=True)
    response = jnp.sum(shares.astype(F32), axis=0)
    return (new_amps, new_resp, response)


def solution(mesh):
    in_specs = (
        P(("wide", "narrow"), None, None),
        P(("wide", "narrow"), None, None),
        P(("wide", "narrow"), None, None),
        P(("wide", "narrow"), None, None),
        P(("wide", "narrow"), None),
        P(("wide", "narrow"), None),
        P(("wide", "narrow"), None),
        P(),
        P(None, "narrow"),
    )
    out_specs = (
        P(("wide", "narrow"), None, None),
        P(("wide", "narrow"), None, None),
        P("wide", "narrow"),
    )
    return jax.shard_map(
        per_device, mesh=mesh, in_specs=in_specs, out_specs=out_specs, check_vma=False
    )
```

```python
import functools

import jax
import jax.numpy as jnp
from jax import lax
from jax.experimental import pallas as pl
from jax.experimental.pallas import tpu as pltpu
from jax.sharding import PartitionSpec as P

BF16 = jnp.bfloat16
F32 = jnp.float32
SMEM = pl.BlockSpec(memory_space=pltpu.SMEM)
VMEM = pl.BlockSpec(memory_space=pltpu.VMEM)
ANY = pl.BlockSpec(memory_space=pl.ANY)
HBM = pl.BlockSpec(memory_space=pltpu.HBM)


def swap(value, wide_mask, narrow_mask, among=None):
    wide, narrow = lax.axis_size("wide"), lax.axis_size("narrow")
    pairs = [
        (i * narrow + j, (i ^ wide_mask) * narrow + (j ^ narrow_mask))
        for i in (among or range(wide))
        for j in range(narrow)
    ]
    return lax.ppermute(value, ("wide", "narrow"), pairs)


def call(kernel, out_shape, specs, micros, *args, scratch=(), out_specs=None, limit=32):
    return pl.pallas_call(
        kernel,
        out_shape=out_shape,
        in_specs=specs,
        out_specs=out_specs or jax.tree.map(lambda _: VMEM, out_shape),
        scratch_shapes=scratch,
        cost_estimate=pl.CostEstimate(flops=int(micros * 1e9), bytes_accessed=0, transcendentals=0),
        compiler_params=pltpu.CompilerParams(vmem_limit_bytes=limit * 1024 * 1024),
    )(*args)


def join_kernel(amps_ref, resp_ref, out_ref, sems):
    npno = amps_ref.shape[1]
    copies = []
    for i, ref in enumerate((amps_ref, resp_ref)):
        copy = pltpu.make_async_copy(ref, out_ref.at[:, :, pl.ds(i * npno, npno)], sems.at[i])
        copy.start()
        copies.append(copy)
    for copy in copies:
        copy.wait()


def pack_kernel(blk, readers_ref, couple_ref, q_ref, after_ref, out_ref):
    del after_ref
    pairs, nfun, npno = q_ref.shape
    count = (out_ref.shape[1] - nfun) // 2
    row = lax.broadcasted_iota(jnp.int32, (count, npno), 0)
    for p in range(pairs):
        for a in range(nfun // blk):
            rows = slice(a * blk, (a + 1) * blk)
            out_ref[p, rows, :] = q_ref[p, rows, :].T
        c = jnp.zeros((count, npno), F32)
        for r in range(readers_ref.shape[1]):
            c = c + jnp.where(row == readers_ref[p, r], couple_ref[p, r], 0.0)
        high = c.astype(BF16)
        out_ref[p, nfun : nfun + count, :] = high
        out_ref[p, nfun + count :, :] = (c - high.astype(F32)).astype(BF16)


def beside_kernel(*refs):
    *in_refs, _, out_ref = refs
    count = in_refs[0].shape[0]
    for i, ref in enumerate(in_refs):
        out_ref[i * count : (i + 1) * count] = ref[...]


def mark_kernel(after_ref, out_ref):
    del after_ref
    out_ref[...] = jnp.zeros_like(out_ref)


def again_kernel(value_ref, after_ref, out_ref):
    del after_ref
    out_ref[...] = value_ref[...]


def load_coefficients(pack_ref, c_ref):
    count = c_ref.shape[1]
    nfun = pack_ref.shape[1] - 2 * count
    for p in range(pack_ref.shape[0]):
        c_ref[p] = pack_ref[p, nfun : nfun + count, :].astype(F32) + pack_ref[p, nfun + count :, :].astype(F32)


def add_terms(sums, overlaps, tz_ref, c_ref, dev):
    pairs, npno, _ = tz_ref.shape
    half = []
    for p, s in enumerate(overlaps):
        h = jnp.dot(s, tz_ref[p], preferred_element_type=F32)
        scaled = []
        for g in range(pairs):
            c = c_ref[g, pl.ds(dev * pairs + p, 1), :]
            c = jnp.concatenate([c, c], axis=1)
            scaled.append((h[g * npno : (g + 1) * npno] * c).astype(BF16))
        half.append(scaled)
    for g in range(pairs):
        rows = slice(g * npno, (g + 1) * npno)
        right = jnp.concatenate([s[rows] for s in overlaps], axis=1)
        left = jnp.concatenate(
            [jnp.concatenate([h[g][:, i * npno : (i + 1) * npno] for h in half], axis=1) for i in range(2)], axis=0
        )
        term = lax.dot_general(left, right, (((1,), (1,)), ((), ())), preferred_element_type=F32)
        sums[g] = term if sums[g] is None else sums[g] + term


def couple_kernel(masks, ahead, blk, narrow, flip, prior, *refs):
    where_ref, dom_ref, pack_ref = refs[:3]
    refs = refs[3:]
    q_refs, refs = refs[: len(masks) + len(ahead)], refs[len(masks) + len(ahead) :]
    tz_refs, refs = refs[: len(masks)], refs[len(masks) :]
    prior_ref, refs = (refs[0], refs[1:]) if prior else (None, refs)
    out_ref, spread_ref, c_ref = refs[0], refs[-2], refs[-1]
    pairs, _, npno = q_refs[0].shape
    dom_blk = q_refs[0].shape[1] // blk
    load_coefficients(pack_ref, c_ref)
    spread_ref[...] = jnp.zeros_like(spread_ref)
    for p in range(pairs):
        pair = ((where_ref[0] ^ flip) * narrow + where_ref[1]) * pairs + p
        for a in range(dom_blk):
            spread_ref[dom_ref[pair * dom_blk + a], p * npno : (p + 1) * npno, :] = pack_ref[
                p, a * blk : (a + 1) * blk, :
            ]
    sums = [prior_ref[g] if prior else None for g in range(pairs)]
    for k, mask in enumerate(masks + ahead):
        dev = where_ref[0] ^ mask
        overlaps = []
        for p in range(pairs):
            pair = (dev * narrow + where_ref[1]) * pairs + p
            left = jnp.concatenate([spread_ref[dom_ref[pair * dom_blk + b]] for b in range(dom_blk)], axis=1)
            overlaps.append(jnp.dot(left, q_refs[k][p], preferred_element_type=F32).astype(BF16))
        if k < len(masks):
            add_terms(sums, overlaps, tz_refs[k], c_ref, dev)
        else:
            for p in range(pairs):
                refs[1][(k - len(masks)) * pairs + p] = overlaps[p]
    for g in range(pairs):
        out_ref[g] = sums[g].astype(out_ref.dtype)


def finish_kernel(masks, *refs):
    where_ref, pack_ref, overlap_ref, prior_ref = refs[:4]
    tz_refs, (out_ref, c_ref) = refs[4 : 4 + len(masks)], refs[4 + len(masks) :]
    pairs = pack_ref.shape[0]
    load_coefficients(pack_ref, c_ref)
    sums = [prior_ref[g] for g in range(pairs)]
    for k, mask in enumerate(masks):
        overlaps = [overlap_ref[k * pairs + p] for p in range(pairs)]
        add_terms(sums, overlaps, tz_refs[k], c_ref, where_ref[0] ^ mask)
    for g in range(pairs):
        out_ref[g] = sums[g].astype(out_ref.dtype)


def update_kernel(
    own_ref, back_ref, amps_ref, resp_ref, ints_ref, energy_ref, after_ref, new_amps_ref, new_resp_ref, w_ref
):
    del after_ref
    npno = amps_ref.shape[1]
    for p in range(amps_ref.shape[0]):
        across = jnp.broadcast_to(energy_ref[pl.ds(p, 1), :], (npno, npno))
        denom = across + across.T
        amps = amps_ref[p].astype(F32)
        resp = resp_ref[p].astype(F32)
        coupled_t = own_ref[p, :npno] + back_ref[p, :npno].astype(F32)
        coupled_z = own_ref[p, npno:] + back_ref[p, npno:].astype(F32)
        new_amps = amps - 0.5 * (ints_ref[p].astype(F32) + denom * amps + coupled_t) / denom
        new_resp = resp - 0.5 * (amps + denom * resp + coupled_z) / denom
        new_amps_ref[p] = new_amps
        new_resp_ref[p] = new_resp
        prod = lax.dot_general(
            new_amps.astype(BF16), new_resp.astype(BF16), (((1,), (1,)), ((), ())), preferred_element_type=F32
        )
        w_ref[p] = (0.5 * (prod + prod.T)).astype(BF16)


def place_kernel(blk, narrow, pairs, *refs):
    where_ref, dom_ref, ints_ref = refs[:3]
    q_refs, (full_ref, moved_ref) = refs[3 : 3 + narrow], refs[4 + narrow :]
    both, nfun, npno = q_refs[0].shape
    dom_blk = nfun // blk
    trash, rows = full_ref.shape[0] - 1, full_ref.shape[1]
    full_ref[...] = jnp.zeros_like(full_ref)
    for k in range(narrow):
        for i in range(both):
            pair = ((where_ref[0] ^ (i // pairs)) * narrow + (where_ref[1] ^ k)) * pairs + i % pairs
            slot = k * both + i
            blocks = []
            for a in range(dom_blk):
                f = dom_ref[pair * dom_blk + a]
                for j in range(blk // rows):
                    dev = f * (blk // rows) + j
                    at = jnp.where((dev ^ where_ref[0]) & 1, trash, dev // 2)
                    start = a * blk + j * rows
                    full_ref[at, :, slot * npno : (slot + 1) * npno] = q_refs[k][i, start : start + rows, :]
                blocks.append(ints_ref[f])
            moved_ref[slot] = lax.dot_general(
                q_refs[k][i], jnp.concatenate(blocks, axis=0), (((0,), (0,)), ((), ())), preferred_element_type=F32
            ).astype(BF16)


def response_kernel(others, narrow, *refs):
    where_ref, full_ref, moved_ref, near_w_ref, core_w_ref = refs[:5]
    out_refs, sum_ref = refs[5:-1], refs[-1]
    slots = moved_ref.shape[0]
    both = slots // narrow
    parts = []
    for slot in range(slots):
        k, i = slot // both, slot % both
        w = (core_w_ref if k % 2 else near_w_ref)[k // 2 * both + i]
        parts.append(jnp.dot(w, moved_ref[slot], preferred_element_type=F32).astype(BF16))
    right = jnp.concatenate(parts, axis=0)
    devs, rows, depth = sum_ref.shape[0], full_ref.shape[1], full_ref.shape[2]
    total = jnp.dot(full_ref[:devs].reshape(devs * rows, depth), right, preferred_element_type=F32)
    sum_ref[...] = total.reshape(sum_ref.shape)
    for mask, out_ref in zip([0] + others, out_refs):
        out_ref[...] = sum_ref[(where_ref[0] ^ mask) // 2].astype(out_ref.dtype)


def sum_kernel(*refs):
    *in_refs, _, out_ref = refs
    out_ref[...] = sum(ref[...].astype(F32) for ref in in_refs)


def per_device(amps, resp, trans, ints, energies, couple, readers, domains, integrals):
    wide, narrow = lax.axis_size("wide"), lax.axis_size("narrow")
    pairs, nfun, npno = trans.shape
    blk = nfun // domains.shape[1]
    nbas, cols = integrals.shape
    near = wide // 2
    partner = wide - 2
    sds = jax.ShapeDtypeStruct

    count = wide * pairs
    where = jnp.stack([lax.axis_index("wide"), lax.axis_index("narrow")]).astype(jnp.int32)
    dom = domains.reshape(-1)

    near_q, near_tz = {0: trans}, {}
    near_q[1] = swap(trans, 1, 0)
    for mask in range(2, near, 2):
        near_q[mask] = swap(trans, mask, 0)
    near_tz[0] = call(
        join_kernel, sds((pairs, npno, 2 * npno), BF16), [ANY, ANY], 1, amps, resp, scratch=[pltpu.SemaphoreType.DMA((2,))]
    )
    near_tz[1] = swap(near_tz[0], 1, 0)
    for mask in range(2, near, 2):
        near_tz[mask] = swap(near_tz[0], mask, 0)
    pack = call(
        functools.partial(pack_kernel, blk),
        sds((pairs, nfun + 2 * count, npno), BF16),
        [SMEM, SMEM, VMEM, ANY], 1,
        readers, couple, trans, near_q[near - 2],
    )
    far_pack = swap(pack, partner, 0)
    for mask in range(2, near, 2):
        near_q[mask + 1] = swap(near_q[mask], 1, 0)
        near_tz[mask + 1] = swap(near_tz[mask], 1, 0)
    early = [0, 1] + list(range(2, near, 2))
    late = list(range(3, near, 2))
    scratch = [
        pltpu.VMEM((nbas // blk, pairs * npno, blk), BF16),
        pltpu.VMEM((pairs, count, npno), F32),
    ]
    sums = sds((pairs, 2 * npno, npno), F32)
    own = call(
        functools.partial(couple_kernel, early, [], blk, narrow, 0, False),
        sums,
        [SMEM] * 2 + [VMEM] * (1 + 2 * len(early)), 2,
        where, dom, pack, *[near_q[m] for m in early], *[near_tz[m] for m in early],
        scratch=scratch,
    )
    far, overlap = call(
        functools.partial(couple_kernel, early, late, blk, narrow, partner, False),
        (sums, sds((len(late) * pairs, pairs * npno, npno), BF16)),
        [SMEM] * 2 + [VMEM] * (1 + 2 * len(early) + len(late)), 3,
        where, dom, far_pack, *[near_q[m] for m in early + late], *[near_tz[m] for m in early],
        scratch=scratch,
    )
    far = call(
        functools.partial(finish_kernel, late),
        sds(sums.shape, BF16),
        [SMEM] + [VMEM] * (3 + len(late)), 1,
        where, far_pack, overlap, far, *[near_tz[m] for m in late],
        scratch=scratch[1:],
    )
    back = swap(far, partner, 0)
    own_late = call(
        functools.partial(couple_kernel, late, [], blk, narrow, 0, True),
        sums,
        [SMEM] * 2 + [VMEM] * (2 + 2 * len(late)), 2,
        where, dom, pack, *[near_q[m] for m in late], *[near_tz[m] for m in late], own,
        scratch=scratch,
    )
    both_q = call(
        beside_kernel, sds((2 * pairs, nfun, npno), BF16), [VMEM] * 2 + [ANY], 0.3, trans, near_q[1], near_tz[1]
    )
    core_q = swap(both_q, 0, 1)
    mats = sds((pairs, npno, npno), F32)
    new_amps, new_resp, weights = call(
        update_kernel,
        (mats, mats, sds((pairs, npno, npno), BF16)),
        [VMEM] * 6 + [ANY], 1,
        own_late, back, amps, resp, ints, energies, core_q,
    )
    narrow_q = {0: both_q, 1: core_q}
    for mask in range(2, narrow, 2):
        arrived = swap(both_q, 0, mask)
        narrow_q[mask] = call(again_kernel, sds(both_q.shape, BF16), [VMEM, ANY], 0.3, arrived, weights)
        narrow_q[mask + 1] = swap(narrow_q[mask], 0, 1)
    slots = 2 * narrow * pairs
    full, moved = call(
        functools.partial(place_kernel, blk, narrow, pairs),
        (sds((near + 1, nbas // wide, slots * npno), BF16), sds((slots, npno, cols), BF16)),
        [SMEM, SMEM] + [VMEM] * (1 + narrow) + [ANY], 1,
        where, dom, integrals.reshape(nbas // blk, blk, cols), *[narrow_q[k] for k in range(narrow)], weights,
    )
    group = [(bit, mask) for mask in range(0, narrow, 2) for bit in range(2)]
    arrived = {key: swap(weights, *key) if any(key) else weights for key in sorted(group, reverse=True)}
    near_w = call(
        beside_kernel, sds((len(group) * pairs, npno, npno), BF16), [VMEM] * len(group) + [ANY], 0.3,
        *[arrived[key] for key in group], moved,
    )
    core_w = swap(near_w, 0, 1)
    others = list(range(wide - 2, 0, -2))
    block = (nbas // wide, cols)
    shares = call(
        functools.partial(response_kernel, others, narrow),
        (sds(block, F32),) + (sds(block, BF16),) * len(others),
        [SMEM] + [VMEM] * 4, 1,
        where, full, moved, near_w, core_w,
        scratch=[pltpu.VMEM((near,) + block, F32)],
    )
    received = [swap(share, mask, 0) for mask, share in zip(others, shares[1:])]
    mark = call(mark_kernel, sds((8, 128), F32), [ANY], 0.1, received[0])
    response = call(
        sum_kernel, sds(block, F32), [VMEM] * (1 + len(others)) + [ANY], 0.1, shares[0], *received, mark
    )
    return (new_amps, new_resp, response)


def solution(mesh):
    in_specs = (
        P(("wide", "narrow"), None, None),
        P(("wide", "narrow"), None, None),
        P(("wide", "narrow"), None, None),
        P(("wide", "narrow"), None, None),
        P(("wide", "narrow"), None),
        P(("wide", "narrow"), None),
        P(("wide", "narrow"), None),
        P(),
        P(None, "narrow"),
    )
    out_specs = (
        P(("wide", "narrow"), None, None),
        P(("wide", "narrow"), None, None),
        P("wide", "narrow"),
    )
    return jax.shard_map(
        per_device, mesh=mesh, in_specs=in_specs, out_specs=out_specs, check_vma=False
    )
```

```python
import functools

import jax
import jax.numpy as jnp
from jax import lax
from jax.experimental import pallas as pl
from jax.experimental.pallas import tpu as pltpu
from jax.sharding import PartitionSpec as P

BF16 = jnp.bfloat16
F32 = jnp.float32
SMEM = pl.BlockSpec(memory_space=pltpu.SMEM)
VMEM = pl.BlockSpec(memory_space=pltpu.VMEM)
ANY = pl.BlockSpec(memory_space=pl.ANY)
HBM = pl.BlockSpec(memory_space=pltpu.HBM)


def swap(value, wide_mask, narrow_mask, among=None):
    wide, narrow = lax.axis_size("wide"), lax.axis_size("narrow")
    pairs = [
        (i * narrow + j, (i ^ wide_mask) * narrow + (j ^ narrow_mask))
        for i in (among or range(wide))
        for j in range(narrow)
    ]
    return lax.ppermute(value, ("wide", "narrow"), pairs)


def call(kernel, out_shape, specs, micros, *args, scratch=(), out_specs=None, limit=32):
    return pl.pallas_call(
        kernel,
        out_shape=out_shape,
        in_specs=specs,
        out_specs=out_specs or jax.tree.map(lambda _: VMEM, out_shape),
        scratch_shapes=scratch,
        cost_estimate=pl.CostEstimate(flops=int(micros * 1e9), bytes_accessed=0, transcendentals=0),
        compiler_params=pltpu.CompilerParams(vmem_limit_bytes=limit * 1024 * 1024),
    )(*args)


def join_kernel(amps_ref, resp_ref, out_ref, sems):
    npno = amps_ref.shape[1]
    copies = []
    for i, ref in enumerate((amps_ref, resp_ref)):
        copy = pltpu.make_async_copy(ref, out_ref.at[:, :, pl.ds(i * npno, npno)], sems.at[i])
        copy.start()
        copies.append(copy)
    for copy in copies:
        copy.wait()


def pack_kernel(blk, readers_ref, couple_ref, q_ref, out_ref):
    pairs, nfun, npno = q_ref.shape
    count = (out_ref.shape[1] - nfun) // 2
    row = lax.broadcasted_iota(jnp.int32, (count, npno), 0)
    for p in range(pairs):
        for a in range(nfun // blk):
            rows = slice(a * blk, (a + 1) * blk)
            out_ref[p, rows, :] = q_ref[p, rows, :].T
        c = jnp.zeros((count, npno), F32)
        for r in range(readers_ref.shape[1]):
            c = c + jnp.where(row == readers_ref[p, r], couple_ref[p, r], 0.0)
        high = c.astype(BF16)
        out_ref[p, nfun : nfun + count, :] = high
        out_ref[p, nfun + count :, :] = (c - high.astype(F32)).astype(BF16)


def beside_kernel(places, *refs):
    *in_refs, _, out_ref = refs
    count = in_refs[0].shape[0]
    for i, ref in zip(places, in_refs):
        out_ref[i * count : (i + 1) * count] = ref[...]


def mark_kernel(after_ref, out_ref):
    del after_ref
    out_ref[...] = jnp.zeros_like(out_ref)


def again_kernel(value_ref, after_ref, out_ref):
    del after_ref
    out_ref[...] = value_ref[...]


def load_coefficients(pack_ref, c_ref):
    count = c_ref.shape[1]
    nfun = pack_ref.shape[1] - 2 * count
    for p in range(pack_ref.shape[0]):
        c_ref[p] = pack_ref[p, nfun : nfun + count, :].astype(F32) + pack_ref[p, nfun + count :, :].astype(F32)


def add_terms(sums, overlaps, tz_ref, c_ref, dev):
    pairs, npno, _ = tz_ref.shape
    half = []
    for p, s in enumerate(overlaps):
        h = jnp.dot(s, tz_ref[p], preferred_element_type=F32)
        scaled = []
        for g in range(pairs):
            c = c_ref[g, pl.ds(dev * pairs + p, 1), :]
            c = jnp.concatenate([c, c], axis=1)
            scaled.append((h[g * npno : (g + 1) * npno] * c).astype(BF16))
        half.append(scaled)
    for g in range(pairs):
        rows = slice(g * npno, (g + 1) * npno)
        right = jnp.concatenate([s[rows] for s in overlaps], axis=1)
        left = jnp.concatenate(
            [jnp.concatenate([h[g][:, i * npno : (i + 1) * npno] for h in half], axis=1) for i in range(2)], axis=0
        )
        term = lax.dot_general(left, right, (((1,), (1,)), ((), ())), preferred_element_type=F32)
        sums[g] = term if sums[g] is None else sums[g] + term


def couple_kernel(masks, ahead, blk, narrow, flip, prior, *refs):
    where_ref, dom_ref, pack_ref = refs[:3]
    refs = refs[3:]
    q_refs, refs = refs[: len(masks) + len(ahead)], refs[len(masks) + len(ahead) :]
    tz_refs, refs = refs[: len(masks)], refs[len(masks) :]
    prior_ref, refs = (refs[0], refs[1:]) if prior else (None, refs)
    out_ref, spread_ref, c_ref = refs[0], refs[-2], refs[-1]
    pairs, _, npno = q_refs[0].shape
    dom_blk = q_refs[0].shape[1] // blk
    load_coefficients(pack_ref, c_ref)
    spread_ref[...] = jnp.zeros_like(spread_ref)
    for p in range(pairs):
        pair = ((where_ref[0] ^ flip) * narrow + where_ref[1]) * pairs + p
        for a in range(dom_blk):
            spread_ref[dom_ref[pair * dom_blk + a], p * npno : (p + 1) * npno, :] = pack_ref[
                p, a * blk : (a + 1) * blk, :
            ]
    sums = [prior_ref[g] if prior else None for g in range(pairs)]
    for k, mask in enumerate(masks + ahead):
        dev = where_ref[0] ^ mask
        overlaps = []
        for p in range(pairs):
            pair = (dev * narrow + where_ref[1]) * pairs + p
            left = jnp.concatenate([spread_ref[dom_ref[pair * dom_blk + b]] for b in range(dom_blk)], axis=1)
            overlaps.append(jnp.dot(left, q_refs[k][p], preferred_element_type=F32).astype(BF16))
        if k < len(masks):
            add_terms(sums, overlaps, tz_refs[k], c_ref, dev)
        else:
            for p in range(pairs):
                refs[1][(k - len(masks)) * pairs + p] = overlaps[p]
    for g in range(pairs):
        out_ref[g] = sums[g].astype(out_ref.dtype)


def finish_kernel(masks, *refs):
    where_ref, pack_ref, overlap_ref, prior_ref = refs[:4]
    tz_refs, (out_ref, c_ref) = refs[4 : 4 + len(masks)], refs[4 + len(masks) :]
    pairs = pack_ref.shape[0]
    load_coefficients(pack_ref, c_ref)
    sums = [prior_ref[g] for g in range(pairs)]
    for k, mask in enumerate(masks):
        overlaps = [overlap_ref[k * pairs + p] for p in range(pairs)]
        add_terms(sums, overlaps, tz_refs[k], c_ref, where_ref[0] ^ mask)
    for g in range(pairs):
        out_ref[g] = sums[g].astype(out_ref.dtype)


def update_kernel(
    own_ref, back_ref, amps_ref, resp_ref, ints_ref, energy_ref, after_ref, new_amps_ref, new_resp_ref, w_ref
):
    del after_ref
    npno = amps_ref.shape[1]
    for p in range(amps_ref.shape[0]):
        across = jnp.broadcast_to(energy_ref[pl.ds(p, 1), :], (npno, npno))
        denom = across + across.T
        amps = amps_ref[p].astype(F32)
        resp = resp_ref[p].astype(F32)
        coupled_t = own_ref[p, :npno] + back_ref[p, :npno].astype(F32)
        coupled_z = own_ref[p, npno:] + back_ref[p, npno:].astype(F32)
        new_amps = amps - 0.5 * (ints_ref[p].astype(F32) + denom * amps + coupled_t) / denom
        new_resp = resp - 0.5 * (amps + denom * resp + coupled_z) / denom
        new_amps_ref[p] = new_amps
        new_resp_ref[p] = new_resp
        prod = lax.dot_general(
            new_amps.astype(BF16), new_resp.astype(BF16), (((1,), (1,)), ((), ())), preferred_element_type=F32
        )
        w_ref[p] = (0.5 * (prod + prod.T)).astype(BF16)


def place_kernel(blk, narrow, pairs, *refs):
    where_ref, dom_ref, ints_ref = refs[:3]
    q_refs, (full_ref, moved_ref) = refs[3 : 3 + narrow], refs[4 + narrow :]
    both, nfun, npno = q_refs[0].shape
    dom_blk = nfun // blk
    trash, rows = full_ref.shape[0] - 1, full_ref.shape[1]
    full_ref[...] = jnp.zeros_like(full_ref)
    for k in range(narrow):
        for i in range(both):
            pair = ((where_ref[0] ^ (i // pairs)) * narrow + (where_ref[1] ^ k)) * pairs + i % pairs
            slot = k * both + i
            blocks = []
            for a in range(dom_blk):
                f = dom_ref[pair * dom_blk + a]
                for j in range(blk // rows):
                    dev = f * (blk // rows) + j
                    at = jnp.where((dev ^ where_ref[0]) & 1, trash, dev // 2)
                    start = a * blk + j * rows
                    full_ref[at, :, slot * npno : (slot + 1) * npno] = q_refs[k][i, start : start + rows, :]
                blocks.append(ints_ref[f])
            moved_ref[slot] = lax.dot_general(
                q_refs[k][i], jnp.concatenate(blocks, axis=0), (((0,), (0,)), ((), ())), preferred_element_type=F32
            ).astype(BF16)


def response_kernel(others, narrow, *refs):
    where_ref, full_ref, moved_ref, near_w_ref, core_w_ref = refs[:5]
    out_refs, sum_ref = refs[5:-1], refs[-1]
    slots = moved_ref.shape[0]
    both = slots // narrow
    parts = []
    for slot in range(slots):
        k, i = slot // both, slot % both
        w = (core_w_ref if k % 2 else near_w_ref)[k // 2 * both + i]
        parts.append(jnp.dot(w, moved_ref[slot], preferred_element_type=F32).astype(BF16))
    right = jnp.concatenate(parts, axis=0)
    devs, rows, depth = sum_ref.shape[0], full_ref.shape[1], full_ref.shape[2]
    total = jnp.dot(full_ref[:devs].reshape(devs * rows, depth), right, preferred_element_type=F32)
    sum_ref[...] = total.reshape(sum_ref.shape)
    for mask, out_ref in zip([0] + others, out_refs):
        out_ref[...] = sum_ref[(where_ref[0] ^ mask) // 2].astype(out_ref.dtype)


def sum_kernel(*refs):
    *in_refs, _, out_ref = refs
    out_ref[...] = sum(ref[...].astype(F32) for ref in in_refs)


def per_device(amps, resp, trans, ints, energies, couple, readers, domains, integrals):
    wide, narrow = lax.axis_size("wide"), lax.axis_size("narrow")
    pairs, nfun, npno = trans.shape
    blk = nfun // domains.shape[1]
    nbas, cols = integrals.shape
    near = wide // 2
    partner = wide - 2
    sds = jax.ShapeDtypeStruct

    count = wide * pairs
    where = jnp.stack([lax.axis_index("wide"), lax.axis_index("narrow")]).astype(jnp.int32)
    dom = domains.reshape(-1)

    near_q, near_tz = {0: trans}, {}
    near_q[1] = swap(trans, 1, 0)
    for mask in range(2, near, 2):
        near_q[mask] = swap(trans, mask, 0)
    near_tz[0] = call(
        join_kernel, sds((pairs, npno, 2 * npno), BF16), [ANY, ANY], 1, amps, resp, scratch=[pltpu.SemaphoreType.DMA((2,))]
    )
    near_tz[1] = swap(near_tz[0], 1, 0)
    for mask in range(2, near, 2):
        near_tz[mask] = swap(near_tz[0], mask, 0)
    pack = call(
        functools.partial(pack_kernel, blk),
        sds((pairs, nfun + 2 * count, npno), BF16),
        [SMEM] * 2 + [VMEM], 1,
        readers, couple, trans,
    )
    pack = call(again_kernel, sds(pack.shape, BF16), [VMEM, ANY], 0.3, pack, near_q[near - 2])
    far_pack = swap(pack, partner, 0)
    for mask in range(2, near, 2):
        near_q[mask + 1] = swap(near_q[mask], 1, 0)
        near_tz[mask + 1] = swap(near_tz[mask], 1, 0)
    early = [0, 1] + list(range(2, near, 2))
    late = list(range(3, near, 2))
    scratch = [
        pltpu.VMEM((nbas // blk, pairs * npno, blk), BF16),
        pltpu.VMEM((pairs, count, npno), F32),
    ]
    sums = sds((pairs, 2 * npno, npno), F32)
    own = call(
        functools.partial(couple_kernel, early, [], blk, narrow, 0, False),
        sums,
        [SMEM] * 2 + [VMEM] * (1 + 2 * len(early)), 2,
        where, dom, pack, *[near_q[m] for m in early], *[near_tz[m] for m in early],
        scratch=scratch,
    )
    far, overlap = call(
        functools.partial(couple_kernel, early, late, blk, narrow, partner, False),
        (sums, sds((len(late) * pairs, pairs * npno, npno), BF16)),
        [SMEM] * 2 + [VMEM] * (1 + 2 * len(early) + len(late)), 3,
        where, dom, far_pack, *[near_q[m] for m in early + late], *[near_tz[m] for m in early],
        scratch=scratch,
    )
    far = call(
        functools.partial(finish_kernel, late),
        sds(sums.shape, BF16),
        [SMEM] + [VMEM] * (3 + len(late)), 1,
        where, far_pack, overlap, far, *[near_tz[m] for m in late],
        scratch=scratch[1:],
    )
    back = swap(far, partner, 0)
    own_late = call(
        functools.partial(couple_kernel, late, [], blk, narrow, 0, True),
        sums,
        [SMEM] * 2 + [VMEM] * (2 + 2 * len(late)), 2,
        where, dom, pack, *[near_q[m] for m in late], *[near_tz[m] for m in late], own,
        scratch=scratch,
    )
    both_q = call(
        functools.partial(beside_kernel, range(2)), sds((2 * pairs, nfun, npno), BF16), [VMEM] * 2 + [ANY], 0.3, trans, near_q[1], near_tz[1]
    )
    core_q = swap(both_q, 0, 1)
    mats = sds((pairs, npno, npno), F32)
    new_amps, new_resp, weights = call(
        update_kernel,
        (mats, mats, sds((pairs, npno, npno), BF16)),
        [VMEM] * 6 + [ANY], 1,
        own_late, back, amps, resp, ints, energies, core_q,
    )
    narrow_q = {0: both_q, 1: core_q}
    for mask in range(2, narrow, 2):
        arrived = swap(both_q, 0, mask)
        narrow_q[mask] = call(again_kernel, sds(both_q.shape, BF16), [VMEM, ANY], 0.3, arrived, weights)
        narrow_q[mask + 1] = swap(narrow_q[mask], 0, 1)
    slots = 2 * narrow * pairs
    full, moved = call(
        functools.partial(place_kernel, blk, narrow, pairs),
        (sds((near + 1, nbas // wide, slots * npno), BF16), sds((slots, npno, cols), BF16)),
        [SMEM, SMEM] + [VMEM] * (1 + narrow) + [ANY], 1,
        where, dom, integrals.reshape(nbas // blk, blk, cols), *[narrow_q[k] for k in range(narrow)], weights,
    )
    group = [(bit, mask) for mask in range(0, narrow, 2) for bit in range(2)]
    arrived = [swap(weights, *key) if any(key) else weights for key in reversed(group)]
    near_w = call(
        functools.partial(beside_kernel, range(len(group) - 1, -1, -1)),
        sds((len(group) * pairs, npno, npno), BF16),
        [VMEM] * len(group) + [ANY], 0.3,
        *arrived, moved,
    )
    core_w = swap(near_w, 0, 1)
    others = list(range(wide - 2, 0, -2))
    block = (nbas // wide, cols)
    shares = call(
        functools.partial(response_kernel, others, narrow),
        (sds(block, F32),) + (sds(block, BF16),) * len(others),
        [SMEM] + [VMEM] * 4, 1,
        where, full, moved, near_w, core_w,
        scratch=[pltpu.VMEM((near,) + block, F32)],
    )
    received = [swap(share, mask, 0) for mask, share in zip(others, shares[1:])]
    mark = call(mark_kernel, sds((8, 128), F32), [ANY], 0.1, received[0])
    response = call(
        sum_kernel, sds(block, F32), [VMEM] * (1 + len(others)) + [ANY], 0.1, shares[0], *received, mark
    )
    return (new_amps, new_resp, response)


def solution(mesh):
    in_specs = (
        P(("wide", "narrow"), None, None),
        P(("wide", "narrow"), None, None),
        P(("wide", "narrow"), None, None),
        P(("wide", "narrow"), None, None),
        P(("wide", "narrow"), None),
        P(("wide", "narrow"), None),
        P(("wide", "narrow"), None),
        P(),
        P(None, "narrow"),
    )
    out_specs = (
        P(("wide", "narrow"), None, None),
        P(("wide", "narrow"), None, None),
        P("wide", "narrow"),
    )
    return jax.shard_map(
        per_device, mesh=mesh, in_specs=in_specs, out_specs=out_specs, check_vma=False
    )
```

```python
import functools

import jax
import jax.numpy as jnp
from jax import lax
from jax.experimental import pallas as pl
from jax.experimental.pallas import tpu as pltpu
from jax.sharding import PartitionSpec as P

BF16 = jnp.bfloat16
F32 = jnp.float32
SMEM = pl.BlockSpec(memory_space=pltpu.SMEM)
VMEM = pl.BlockSpec(memory_space=pltpu.VMEM)
ANY = pl.BlockSpec(memory_space=pl.ANY)
HBM = pl.BlockSpec(memory_space=pltpu.HBM)


def swap(value, wide_mask, narrow_mask, among=None):
    wide, narrow = lax.axis_size("wide"), lax.axis_size("narrow")
    pairs = [
        (i * narrow + j, (i ^ wide_mask) * narrow + (j ^ narrow_mask))
        for i in (among or range(wide))
        for j in range(narrow)
    ]
    return lax.ppermute(value, ("wide", "narrow"), pairs)


def call(kernel, out_shape, specs, micros, *args, scratch=(), out_specs=None, limit=32):
    return pl.pallas_call(
        kernel,
        out_shape=out_shape,
        in_specs=specs,
        out_specs=out_specs or jax.tree.map(lambda _: VMEM, out_shape),
        scratch_shapes=scratch,
        cost_estimate=pl.CostEstimate(flops=int(micros * 1e9), bytes_accessed=0, transcendentals=0),
        compiler_params=pltpu.CompilerParams(vmem_limit_bytes=limit * 1024 * 1024),
    )(*args)


def join_kernel(amps_ref, resp_ref, out_ref, sems):
    npno = amps_ref.shape[1]
    copies = []
    for i, ref in enumerate((amps_ref, resp_ref)):
        copy = pltpu.make_async_copy(ref, out_ref.at[:, :, pl.ds(i * npno, npno)], sems.at[i])
        copy.start()
        copies.append(copy)
    for copy in copies:
        copy.wait()


def pack_kernel(blk, readers_ref, couple_ref, q_ref, out_ref):
    pairs, nfun, npno = q_ref.shape
    count = (out_ref.shape[1] - nfun) // 2
    row = lax.broadcasted_iota(jnp.int32, (count, npno), 0)
    for p in range(pairs):
        for a in range(nfun // blk):
            rows = slice(a * blk, (a + 1) * blk)
            out_ref[p, rows, :] = q_ref[p, rows, :].T
        c = jnp.zeros((count, npno), F32)
        for r in range(readers_ref.shape[1]):
            c = c + jnp.where(row == readers_ref[p, r], couple_ref[p, r], 0.0)
        high = c.astype(BF16)
        out_ref[p, nfun : nfun + count, :] = high
        out_ref[p, nfun + count :, :] = (c - high.astype(F32)).astype(BF16)


def beside_kernel(places, *refs):
    *in_refs, _, out_ref = refs
    count = in_refs[0].shape[0]
    for i, ref in zip(places, in_refs):
        out_ref[i * count : (i + 1) * count] = ref[...]


def mark_kernel(*refs):
    refs[-1][...] = jnp.zeros_like(refs[-1])


def again_kernel(value_ref, after_ref, out_ref):
    del after_ref
    out_ref[...] = value_ref[...]


def load_coefficients(pack_ref, c_ref):
    count = c_ref.shape[1]
    nfun = pack_ref.shape[1] - 2 * count
    for p in range(pack_ref.shape[0]):
        c_ref[p] = pack_ref[p, nfun : nfun + count, :].astype(F32) + pack_ref[p, nfun + count :, :].astype(F32)


def add_terms(sums, overlaps, tz_ref, c_ref, dev):
    pairs, npno, _ = tz_ref.shape
    half = []
    for p, s in enumerate(overlaps):
        h = jnp.dot(s, tz_ref[p], preferred_element_type=F32)
        scaled = []
        for g in range(pairs):
            c = c_ref[g, pl.ds(dev * pairs + p, 1), :]
            c = jnp.concatenate([c, c], axis=1)
            scaled.append((h[g * npno : (g + 1) * npno] * c).astype(BF16))
        half.append(scaled)
    for g in range(pairs):
        rows = slice(g * npno, (g + 1) * npno)
        right = jnp.concatenate([s[rows] for s in overlaps], axis=1)
        left = jnp.concatenate(
            [jnp.concatenate([h[g][:, i * npno : (i + 1) * npno] for h in half], axis=1) for i in range(2)], axis=0
        )
        term = lax.dot_general(left, right, (((1,), (1,)), ((), ())), preferred_element_type=F32)
        sums[g] = term if sums[g] is None else sums[g] + term


def couple_kernel(masks, blk, narrow, flip, prior, *refs):
    where_ref, dom_ref, pack_ref = refs[:3]
    refs = refs[3:]
    q_refs, refs = refs[: len(masks)], refs[len(masks) :]
    tz_refs, refs = refs[: len(masks)], refs[len(masks) :]
    prior_ref, refs = (refs[0], refs[1:]) if prior else (None, refs)
    out_ref, spread_ref, c_ref = refs[0], refs[-2], refs[-1]
    pairs, _, npno = q_refs[0].shape
    dom_blk = q_refs[0].shape[1] // blk
    load_coefficients(pack_ref, c_ref)
    spread_ref[...] = jnp.zeros_like(spread_ref)
    for p in range(pairs):
        pair = ((where_ref[0] ^ flip) * narrow + where_ref[1]) * pairs + p
        for a in range(dom_blk):
            spread_ref[dom_ref[pair * dom_blk + a], p * npno : (p + 1) * npno, :] = pack_ref[
                p, a * blk : (a + 1) * blk, :
            ]
    sums = [prior_ref[g] if prior else None for g in range(pairs)]
    for k, mask in enumerate(masks):
        dev = where_ref[0] ^ mask
        overlaps = []
        for p in range(pairs):
            pair = (dev * narrow + where_ref[1]) * pairs + p
            left = jnp.concatenate([spread_ref[dom_ref[pair * dom_blk + b]] for b in range(dom_blk)], axis=1)
            overlaps.append(jnp.dot(left, q_refs[k][p], preferred_element_type=F32).astype(BF16))
        add_terms(sums, overlaps, tz_refs[k], c_ref, dev)
    for g in range(pairs):
        out_ref[g] = sums[g].astype(out_ref.dtype)


def updated(p, own_ref, back_ref, amps_ref, resp_ref, ints_ref, energy_ref):
    npno = amps_ref.shape[1]
    across = jnp.broadcast_to(energy_ref[pl.ds(p, 1), :], (npno, npno))
    denom = across + across.T
    amps = amps_ref[p].astype(F32)
    resp = resp_ref[p].astype(F32)
    coupled_t = own_ref[p, :npno] + back_ref[p, :npno].astype(F32)
    coupled_z = own_ref[p, npno:] + back_ref[p, npno:].astype(F32)
    new_amps = amps - 0.5 * (ints_ref[p].astype(F32) + denom * amps + coupled_t) / denom
    new_resp = resp - 0.5 * (amps + denom * resp + coupled_z) / denom
    return new_amps, new_resp


def weights_kernel(*refs):
    w_ref = refs[-1]
    for p in range(w_ref.shape[0]):
        new_amps, new_resp = updated(p, *refs[:6])
        prod = lax.dot_general(
            new_amps.astype(BF16), new_resp.astype(BF16), (((1,), (1,)), ((), ())), preferred_element_type=F32
        )
        w_ref[p] = (0.5 * (prod + prod.T)).astype(BF16)


def update_kernel(*refs):
    new_amps_ref, new_resp_ref, done_ref = refs[-3:]
    for p in range(new_amps_ref.shape[0]):
        new_amps_ref[p], new_resp_ref[p] = updated(p, *refs[:6])
    done_ref[...] = jnp.zeros_like(done_ref)


def place_kernel(blk, narrow, pairs, *refs):
    where_ref, dom_ref, ints_ref = refs[:3]
    q_refs, (full_ref, moved_ref) = refs[3 : 3 + narrow], refs[4 + narrow :]
    both, nfun, npno = q_refs[0].shape
    dom_blk = nfun // blk
    trash, rows = full_ref.shape[0] - 1, full_ref.shape[1]
    full_ref[...] = jnp.zeros_like(full_ref)
    for k in range(narrow):
        for i in range(both):
            pair = ((where_ref[0] ^ (i // pairs)) * narrow + (where_ref[1] ^ k)) * pairs + i % pairs
            slot = k * both + i
            blocks = []
            for a in range(dom_blk):
                f = dom_ref[pair * dom_blk + a]
                for j in range(blk // rows):
                    dev = f * (blk // rows) + j
                    at = jnp.where((dev ^ where_ref[0]) & 1, trash, dev // 2)
                    start = a * blk + j * rows
                    full_ref[at, :, slot * npno : (slot + 1) * npno] = q_refs[k][i, start : start + rows, :]
                blocks.append(ints_ref[f])
            moved_ref[slot] = lax.dot_general(
                q_refs[k][i], jnp.concatenate(blocks, axis=0), (((0,), (0,)), ((), ())), preferred_element_type=F32
            ).astype(BF16)


def response_kernel(others, narrow, *refs):
    where_ref, full_ref, moved_ref, near_w_ref, core_w_ref = refs[:5]
    out_refs, sum_ref = refs[5:-1], refs[-1]
    slots = moved_ref.shape[0]
    both = slots // narrow
    parts = []
    for slot in range(slots):
        k, i = slot // both, slot % both
        w = (core_w_ref if k % 2 else near_w_ref)[k // 2 * both + i]
        parts.append(jnp.dot(w, moved_ref[slot], preferred_element_type=F32).astype(BF16))
    right = jnp.concatenate(parts, axis=0)
    devs, rows, depth = sum_ref.shape[0], full_ref.shape[1], full_ref.shape[2]
    total = jnp.dot(full_ref[:devs].reshape(devs * rows, depth), right, preferred_element_type=F32)
    sum_ref[...] = total.reshape(sum_ref.shape)
    for mask, out_ref in zip([0] + others, out_refs):
        out_ref[...] = sum_ref[(where_ref[0] ^ mask) // 2].astype(out_ref.dtype)


def sum_kernel(*refs):
    *in_refs, _, out_ref = refs
    out_ref[...] = sum(ref[...].astype(F32) for ref in in_refs)


def per_device(amps, resp, trans, ints, energies, couple, readers, domains, integrals):
    wide, narrow = lax.axis_size("wide"), lax.axis_size("narrow")
    pairs, nfun, npno = trans.shape
    blk = nfun // domains.shape[1]
    nbas, cols = integrals.shape
    near = wide // 2
    partner = wide - 2
    sds = jax.ShapeDtypeStruct

    count = wide * pairs
    where = jnp.stack([lax.axis_index("wide"), lax.axis_index("narrow")]).astype(jnp.int32)
    dom = domains.reshape(-1)

    near_q, near_tz = {0: trans}, {}
    near_q[1] = swap(trans, 1, 0)
    for mask in range(2, near, 2):
        near_q[mask] = swap(trans, mask, 0)
    near_tz[0] = call(
        join_kernel, sds((pairs, npno, 2 * npno), BF16), [ANY, ANY], 1, amps, resp, scratch=[pltpu.SemaphoreType.DMA((2,))]
    )
    near_tz[1] = swap(near_tz[0], 1, 0)
    for mask in range(2, near, 2):
        near_tz[mask] = swap(near_tz[0], mask, 0)
    pack = call(
        functools.partial(pack_kernel, blk),
        sds((pairs, nfun + 2 * count, npno), BF16),
        [SMEM] * 2 + [VMEM], 1,
        readers, couple, trans,
    )
    pack = call(again_kernel, sds(pack.shape, BF16), [VMEM, ANY], 0.3, pack, near_q[near - 2])
    far_pack = swap(pack, partner, 0)
    for mask in range(2, near, 2):
        near_q[mask + 1] = swap(near_q[mask], 1, 0)
        near_tz[mask + 1] = swap(near_tz[mask], 1, 0)
    early = [0, 1] + list(range(2, near, 2))
    late = list(range(3, near, 2))
    scratch = [
        pltpu.VMEM((nbas // blk, pairs * npno, blk), BF16),
        pltpu.VMEM((pairs, count, npno), F32),
    ]
    sums = sds((pairs, 2 * npno, npno), F32)
    own = call(
        functools.partial(couple_kernel, early, blk, narrow, 0, False),
        sums,
        [SMEM] * 2 + [VMEM] * (1 + 2 * len(early)), 2,
        where, dom, pack, *[near_q[m] for m in early], *[near_tz[m] for m in early],
        scratch=scratch,
    )
    far = call(
        functools.partial(couple_kernel, early + late, blk, narrow, partner, False),
        sds(sums.shape, BF16),
        [SMEM] * 2 + [VMEM] * (1 + 2 * near), 4,
        where, dom, far_pack, *[near_q[m] for m in early + late], *[near_tz[m] for m in early + late],
        scratch=scratch,
    )
    back = swap(far, partner, 0)
    own_late = call(
        functools.partial(couple_kernel, late, blk, narrow, 0, True),
        sums,
        [SMEM] * 2 + [VMEM] * (2 + 2 * len(late)), 2,
        where, dom, pack, *[near_q[m] for m in late], *[near_tz[m] for m in late], own,
        scratch=scratch,
    )
    both_q = call(
        functools.partial(beside_kernel, range(2)), sds((2 * pairs, nfun, npno), BF16), [VMEM] * 2 + [ANY], 0.3, trans, near_q[1], near_tz[1]
    )
    core_q = swap(both_q, 0, 1)
    mats = sds((pairs, npno, npno), F32)
    state = (own_late, back, amps, resp, ints, energies)
    weights = call(weights_kernel, sds((pairs, npno, npno), BF16), [VMEM] * 6 + [ANY], 1, *state, core_q)
    token = sds((8, 128), F32)
    new_amps, new_resp, done = call(update_kernel, (mats, mats, token), [VMEM] * 6 + [ANY], 1, *state, weights)
    narrow_q = {0: both_q, 1: core_q}
    for mask in range(2, narrow, 2):
        arrived = swap(both_q, 0, mask)
        narrow_q[mask] = call(again_kernel, sds(both_q.shape, BF16), [VMEM, ANY], 0.3, arrived, weights)
        narrow_q[mask + 1] = swap(narrow_q[mask], 0, 1)
    slots = 2 * narrow * pairs
    full, moved = call(
        functools.partial(place_kernel, blk, narrow, pairs),
        (sds((near + 1, nbas // wide, slots * npno), BF16), sds((slots, npno, cols), BF16)),
        [SMEM, SMEM] + [VMEM] * (1 + narrow) + [ANY], 1,
        where, dom, integrals.reshape(nbas // blk, blk, cols), *[narrow_q[k] for k in range(narrow)], weights,
    )
    group = [(bit, mask) for mask in range(0, narrow, 2) for bit in range(2)]
    arrived = [swap(weights, *key) if any(key) else weights for key in reversed(group)]
    near_w = call(
        functools.partial(beside_kernel, range(len(group) - 1, -1, -1)),
        sds((len(group) * pairs, npno, npno), BF16),
        [VMEM] * len(group) + [ANY], 0.3,
        *arrived, moved,
    )
    core_w = swap(near_w, 0, 1)
    others = list(range(wide - 2, 0, -2))
    block = (nbas // wide, cols)
    shares = call(
        functools.partial(response_kernel, others, narrow),
        (sds(block, F32),) + (sds(block, BF16),) * len(others),
        [SMEM] + [VMEM] * 4, 1,
        where, full, moved, near_w, core_w,
        scratch=[pltpu.VMEM((near,) + block, F32)],
    )
    received = [swap(share, mask, 0) for mask, share in zip(others, shares[1:])]
    mark = call(mark_kernel, token, [ANY] * 2, 0.1, received[0], done)
    response = call(
        sum_kernel, sds(block, F32), [VMEM] * (1 + len(others)) + [ANY], 0.1, shares[0], *received, mark
    )
    return (new_amps, new_resp, response)


def solution(mesh):
    in_specs = (
        P(("wide", "narrow"), None, None),
        P(("wide", "narrow"), None, None),
        P(("wide", "narrow"), None, None),
        P(("wide", "narrow"), None, None),
        P(("wide", "narrow"), None),
        P(("wide", "narrow"), None),
        P(("wide", "narrow"), None),
        P(),
        P(None, "narrow"),
    )
    out_specs = (
        P(("wide", "narrow"), None, None),
        P(("wide", "narrow"), None, None),
        P("wide", "narrow"),
    )
    return jax.shard_map(
        per_device, mesh=mesh, in_specs=in_specs, out_specs=out_specs, check_vma=False
    )
```

```python
import functools

import jax
import jax.numpy as jnp
from jax import lax
from jax.experimental import pallas as pl
from jax.experimental.pallas import tpu as pltpu
from jax.sharding import PartitionSpec as P

BF16 = jnp.bfloat16
F32 = jnp.float32
SMEM = pl.BlockSpec(memory_space=pltpu.SMEM)
VMEM = pl.BlockSpec(memory_space=pltpu.VMEM)
ANY = pl.BlockSpec(memory_space=pl.ANY)
HBM = pl.BlockSpec(memory_space=pltpu.HBM)


def swap(value, wide_mask, narrow_mask, among=None):
    wide, narrow = lax.axis_size("wide"), lax.axis_size("narrow")
    pairs = [
        (i * narrow + j, (i ^ wide_mask) * narrow + (j ^ narrow_mask))
        for i in (among or range(wide))
        for j in range(narrow)
    ]
    return lax.ppermute(value, ("wide", "narrow"), pairs)


def call(kernel, out_shape, specs, micros, *args, scratch=(), out_specs=None, limit=32):
    return pl.pallas_call(
        kernel,
        out_shape=out_shape,
        in_specs=specs,
        out_specs=out_specs or jax.tree.map(lambda _: VMEM, out_shape),
        scratch_shapes=scratch,
        cost_estimate=pl.CostEstimate(flops=int(micros * 1e9), bytes_accessed=0, transcendentals=0),
        compiler_params=pltpu.CompilerParams(vmem_limit_bytes=limit * 1024 * 1024),
    )(*args)


def join_kernel(amps_ref, resp_ref, out_ref, sems):
    npno = amps_ref.shape[1]
    copies = []
    for i, ref in enumerate((amps_ref, resp_ref)):
        copy = pltpu.make_async_copy(ref, out_ref.at[:, :, pl.ds(i * npno, npno)], sems.at[i])
        copy.start()
        copies.append(copy)
    for copy in copies:
        copy.wait()


def pack_kernel(blk, readers_ref, couple_ref, q_ref, out_ref):
    pairs, nfun, npno = q_ref.shape
    count = (out_ref.shape[1] - nfun) // 2
    row = lax.broadcasted_iota(jnp.int32, (count, npno), 0)
    for p in range(pairs):
        for a in range(nfun // blk):
            rows = slice(a * blk, (a + 1) * blk)
            out_ref[p, rows, :] = q_ref[p, rows, :].T
        c = jnp.zeros((count, npno), F32)
        for r in range(readers_ref.shape[1]):
            c = c + jnp.where(row == readers_ref[p, r], couple_ref[p, r], 0.0)
        high = c.astype(BF16)
        out_ref[p, nfun : nfun + count, :] = high
        out_ref[p, nfun + count :, :] = (c - high.astype(F32)).astype(BF16)


def beside_kernel(places, *refs):
    *in_refs, _, out_ref = refs
    count = in_refs[0].shape[0]
    for i, ref in zip(places, in_refs):
        out_ref[i * count : (i + 1) * count] = ref[...]


def mark_kernel(*refs):
    refs[-1][...] = jnp.zeros_like(refs[-1])


def again_kernel(value_ref, after_ref, out_ref):
    del after_ref
    out_ref[...] = value_ref[...]


def load_coefficients(pack_ref, c_ref):
    count = c_ref.shape[1]
    nfun = pack_ref.shape[1] - 2 * count
    for p in range(pack_ref.shape[0]):
        c_ref[p] = pack_ref[p, nfun : nfun + count, :].astype(F32) + pack_ref[p, nfun + count :, :].astype(F32)


def add_terms(sums, overlaps, tz_ref, c_ref, dev):
    pairs, npno, _ = tz_ref.shape
    half = []
    for p, s in enumerate(overlaps):
        h = jnp.dot(s, tz_ref[p], preferred_element_type=F32)
        scaled = []
        for g in range(pairs):
            c = c_ref[g, pl.ds(dev * pairs + p, 1), :]
            c = jnp.concatenate([c, c], axis=1)
            scaled.append((h[g * npno : (g + 1) * npno] * c).astype(BF16))
        half.append(scaled)
    for g in range(pairs):
        rows = slice(g * npno, (g + 1) * npno)
        right = jnp.concatenate([s[rows] for s in overlaps], axis=1)
        left = jnp.concatenate(
            [jnp.concatenate([h[g][:, i * npno : (i + 1) * npno] for h in half], axis=1) for i in range(2)], axis=0
        )
        term = lax.dot_general(left, right, (((1,), (1,)), ((), ())), preferred_element_type=F32)
        sums[g] = term if sums[g] is None else sums[g] + term


def couple_kernel(masks, blk, narrow, flip, prior, *refs):
    where_ref, dom_ref, pack_ref = refs[:3]
    refs = refs[3:]
    q_refs, refs = refs[: len(masks)], refs[len(masks) :]
    tz_refs, refs = refs[: len(masks)], refs[len(masks) :]
    prior_ref, refs = (refs[0], refs[1:]) if prior else (None, refs)
    out_ref, spread_ref, c_ref = refs[0], refs[-2], refs[-1]
    pairs, _, npno = q_refs[0].shape
    dom_blk = q_refs[0].shape[1] // blk
    load_coefficients(pack_ref, c_ref)
    spread_ref[...] = jnp.zeros_like(spread_ref)
    for p in range(pairs):
        pair = ((where_ref[0] ^ flip) * narrow + where_ref[1]) * pairs + p
        for a in range(dom_blk):
            spread_ref[dom_ref[pair * dom_blk + a], p * npno : (p + 1) * npno, :] = pack_ref[
                p, a * blk : (a + 1) * blk, :
            ]
    sums = [prior_ref[g] if prior else None for g in range(pairs)]
    for k, mask in enumerate(masks):
        dev = where_ref[0] ^ mask
        overlaps = []
        for p in range(pairs):
            pair = (dev * narrow + where_ref[1]) * pairs + p
            left = jnp.concatenate([spread_ref[dom_ref[pair * dom_blk + b]] for b in range(dom_blk)], axis=1)
            overlaps.append(jnp.dot(left, q_refs[k][p], preferred_element_type=F32).astype(BF16))
        add_terms(sums, overlaps, tz_refs[k], c_ref, dev)
    for g in range(pairs):
        out_ref[g] = sums[g].astype(out_ref.dtype)


def updated(p, own_ref, back_ref, amps_ref, resp_ref, ints_ref, energy_ref):
    npno = amps_ref.shape[1]
    across = jnp.broadcast_to(energy_ref[pl.ds(p, 1), :], (npno, npno))
    denom = across + across.T
    amps = amps_ref[p].astype(F32)
    resp = resp_ref[p].astype(F32)
    coupled_t = own_ref[p, :npno] + back_ref[p, :npno].astype(F32)
    coupled_z = own_ref[p, npno:] + back_ref[p, npno:].astype(F32)
    new_amps = amps - 0.5 * (ints_ref[p].astype(F32) + denom * amps + coupled_t) / denom
    new_resp = resp - 0.5 * (amps + denom * resp + coupled_z) / denom
    return new_amps, new_resp


def weights_kernel(*refs):
    w_ref = refs[-1]
    npno = w_ref.shape[2]
    row = lax.broadcasted_iota(jnp.int32, (npno, npno), 0)
    col = lax.broadcasted_iota(jnp.int32, (npno, npno), 1)
    for at in range(w_ref.shape[0]):
        both = []
        for p in (2 * at, 2 * at + 1):
            new_amps, new_resp = updated(p, *refs[:6])
            prod = lax.dot_general(
                new_amps.astype(BF16), new_resp.astype(BF16), (((1,), (1,)), ((), ())), preferred_element_type=F32
            )
            both.append(0.5 * (prod + prod.T))
        w_ref[at, :npno, :] = jnp.where(row <= col, both[0], both[1]).astype(BF16)
        diagonal = jnp.sum(jnp.where(row == col, both[1], 0.0), axis=0, keepdims=True)
        w_ref[at, npno:, :] = jnp.broadcast_to(diagonal, (w_ref.shape[1] - npno, npno)).astype(BF16)


def update_kernel(*refs):
    new_amps_ref, new_resp_ref, done_ref = refs[-3:]
    for p in range(new_amps_ref.shape[0]):
        new_amps_ref[p], new_resp_ref[p] = updated(p, *refs[:6])
    done_ref[...] = jnp.zeros_like(done_ref)


def place_kernel(blk, narrow, pairs, *refs):
    where_ref, dom_ref, ints_ref = refs[:3]
    q_refs, (full_ref, moved_ref) = refs[3 : 3 + narrow], refs[4 + narrow :]
    both, nfun, npno = q_refs[0].shape
    dom_blk = nfun // blk
    trash, rows = full_ref.shape[0] - 1, full_ref.shape[1]
    full_ref[...] = jnp.zeros_like(full_ref)
    for k in range(narrow):
        for i in range(both):
            pair = ((where_ref[0] ^ (i // pairs)) * narrow + (where_ref[1] ^ k)) * pairs + i % pairs
            slot = k * both + i
            blocks = []
            for a in range(dom_blk):
                f = dom_ref[pair * dom_blk + a]
                for j in range(blk // rows):
                    dev = f * (blk // rows) + j
                    apart = dev ^ where_ref[0]
                    at = jnp.where(apart & 1, trash, apart // 2)
                    start = a * blk + j * rows
                    full_ref[at, :, slot * npno : (slot + 1) * npno] = q_refs[k][i, start : start + rows, :]
                blocks.append(ints_ref[f])
            moved_ref[slot] = lax.dot_general(
                q_refs[k][i], jnp.concatenate(blocks, axis=0), (((0,), (0,)), ((), ())), preferred_element_type=F32
            ).astype(BF16)


def unpacked(ref, at):
    npno = ref.shape[2]
    row = lax.broadcasted_iota(jnp.int32, (npno, npno), 0)
    col = lax.broadcasted_iota(jnp.int32, (npno, npno), 1)
    mixed = ref[at, :npno, :]
    upper, lower = mixed.astype(F32), mixed.T.astype(F32)
    diagonal = jnp.broadcast_to(ref[at, npno:, :].astype(F32)[:1], (npno, npno))
    first = jnp.where(row <= col, upper, lower)
    second = jnp.where(row == col, diagonal, jnp.where(row > col, upper, lower))
    return first.astype(BF16), second.astype(BF16)


def half_response(narrow, odd, full_ref, moved_ref, w_ref, total):
    both, npno = moved_ref.shape[0] // narrow, moved_ref.shape[1]
    devs, rows = full_ref.shape[0] - 1, full_ref.shape[1]
    for k in range(odd, narrow, 2):
        parts = []
        for at in range(k // 2 * both // 2, (k // 2 + 1) * both // 2):
            for w in unpacked(w_ref, at):
                moved = moved_ref[k * both + len(parts)]
                parts.append(jnp.dot(w, moved, preferred_element_type=F32).astype(BF16))
        left = full_ref[:devs, :, k * both * npno : (k + 1) * both * npno].reshape(devs * rows, both * npno)
        term = jnp.dot(left, jnp.concatenate(parts, axis=0), preferred_element_type=F32)
        total = term if total is None else total + term
    return total


def near_kernel(narrow, full_ref, moved_ref, w_ref, out_ref):
    out_ref[...] = half_response(narrow, 0, full_ref, moved_ref, w_ref, None).reshape(out_ref.shape)


def response_kernel(others, narrow, *refs):
    full_ref, moved_ref, near_ref, w_ref = refs[:4]
    devs, rows, cols = near_ref.shape
    total = half_response(narrow, 1, full_ref, moved_ref, w_ref, near_ref[...].reshape(devs * rows, cols))
    for mask, out_ref in zip([0] + others, refs[4:]):
        out_ref[...] = total[mask // 2 * rows : (mask // 2 + 1) * rows].astype(out_ref.dtype)


def sum_kernel(*refs):
    *in_refs, _, out_ref = refs
    out_ref[...] = sum(ref[...].astype(F32) for ref in in_refs)


def per_device(amps, resp, trans, ints, energies, couple, readers, domains, integrals):
    wide, narrow = lax.axis_size("wide"), lax.axis_size("narrow")
    pairs, nfun, npno = trans.shape
    blk = nfun // domains.shape[1]
    nbas, cols = integrals.shape
    near = wide // 2
    partner = wide - 2
    sds = jax.ShapeDtypeStruct

    count = wide * pairs
    where = jnp.stack([lax.axis_index("wide"), lax.axis_index("narrow")]).astype(jnp.int32)
    dom = domains.reshape(-1)

    near_q, near_tz = {0: trans}, {}
    near_q[1] = swap(trans, 1, 0)
    for mask in range(2, near, 2):
        near_q[mask] = swap(trans, mask, 0)
    near_tz[0] = call(
        join_kernel, sds((pairs, npno, 2 * npno), BF16), [ANY, ANY], 1, amps, resp, scratch=[pltpu.SemaphoreType.DMA((2,))]
    )
    near_tz[1] = swap(near_tz[0], 1, 0)
    for mask in range(2, near, 2):
        near_tz[mask] = swap(near_tz[0], mask, 0)
    pack = call(
        functools.partial(pack_kernel, blk),
        sds((pairs, nfun + 2 * count, npno), BF16),
        [SMEM] * 2 + [VMEM], 1,
        readers, couple, trans,
    )
    pack = call(again_kernel, sds(pack.shape, BF16), [VMEM, ANY], 0.3, pack, near_q[near - 2])
    far_pack = swap(pack, partner, 0)
    for mask in range(2, near, 2):
        near_q[mask + 1] = swap(near_q[mask], 1, 0)
        near_tz[mask + 1] = swap(near_tz[mask], 1, 0)
    early = [0, 1] + list(range(2, near, 2))
    late = list(range(3, near, 2))
    scratch = [
        pltpu.VMEM((nbas // blk, pairs * npno, blk), BF16),
        pltpu.VMEM((pairs, count, npno), F32),
    ]
    sums = sds((pairs, 2 * npno, npno), F32)
    own = call(
        functools.partial(couple_kernel, early, blk, narrow, 0, False),
        sums,
        [SMEM] * 2 + [VMEM] * (1 + 2 * len(early)), 2,
        where, dom, pack, *[near_q[m] for m in early], *[near_tz[m] for m in early],
        scratch=scratch,
    )
    far = call(
        functools.partial(couple_kernel, early + late, blk, narrow, partner, False),
        sds(sums.shape, BF16),
        [SMEM] * 2 + [VMEM] * (1 + 2 * near), 4,
        where, dom, far_pack, *[near_q[m] for m in early + late], *[near_tz[m] for m in early + late],
        scratch=scratch,
    )
    back = swap(far, partner, 0)
    own_late = call(
        functools.partial(couple_kernel, late, blk, narrow, 0, True),
        sums,
        [SMEM] * 2 + [VMEM] * (2 + 2 * len(late)), 2,
        where, dom, pack, *[near_q[m] for m in late], *[near_tz[m] for m in late], own,
        scratch=scratch,
    )
    both_q = call(
        functools.partial(beside_kernel, range(2)), sds((2 * pairs, nfun, npno), BF16), [VMEM] * 2 + [ANY], 0.3, trans, near_q[1], near_tz[1]
    )
    core_q = swap(both_q, 0, 1)
    mats = sds((pairs, npno, npno), F32)
    state = (own_late, back, amps, resp, ints, energies)
    weights = call(weights_kernel, sds((pairs // 2, npno + 16, npno), BF16), [VMEM] * 6 + [ANY], 1, *state, core_q)
    token = sds((8, 128), F32)
    new_amps, new_resp, done = call(update_kernel, (mats, mats, token), [VMEM] * 6 + [ANY], 1, *state, weights)
    narrow_q = {0: both_q, 1: core_q}
    for mask in range(2, narrow, 2):
        arrived = swap(both_q, 0, mask)
        narrow_q[mask] = call(again_kernel, sds(both_q.shape, BF16), [VMEM, ANY], 0.3, arrived, weights)
        narrow_q[mask + 1] = swap(narrow_q[mask], 0, 1)
    slots = 2 * narrow * pairs
    full, moved = call(
        functools.partial(place_kernel, blk, narrow, pairs),
        (sds((near + 1, nbas // wide, slots * npno), BF16), sds((slots, npno, cols), BF16)),
        [SMEM, SMEM] + [VMEM] * (1 + narrow) + [ANY], 1,
        where, dom, integrals.reshape(nbas // blk, blk, cols), *[narrow_q[k] for k in range(narrow)], weights,
    )
    group = [(bit, mask) for mask in range(0, narrow, 2) for bit in range(2)]
    arrived = [swap(weights, *key) if any(key) else weights for key in reversed(group)]
    near_w = call(
        functools.partial(beside_kernel, range(len(group) - 1, -1, -1)),
        sds((len(group) * pairs // 2, npno + 16, npno), BF16),
        [VMEM] * len(group) + [ANY], 0.3,
        *arrived, moved,
    )
    core_w = swap(near_w, 0, 1)
    near_part = call(
        functools.partial(near_kernel, narrow), sds((near, nbas // wide, cols), F32), [VMEM] * 3, 0.5,
        full, moved, near_w,
    )
    others = list(range(wide - 2, 0, -2))
    block = (nbas // wide, cols)
    shares = call(
        functools.partial(response_kernel, others, narrow),
        (sds(block, F32),) + (sds(block, BF16),) * len(others),
        [VMEM] * 4, 1,
        full, moved, near_part, core_w,
    )
    received = [swap(share, mask, 0) for mask, share in zip(others, shares[1:])]
    mark = call(mark_kernel, token, [ANY] * 2, 0.1, received[0], done)
    response = call(
        sum_kernel, sds(block, F32), [VMEM] * (1 + len(others)) + [ANY], 0.1, shares[0], *received, mark
    )
    return (new_amps, new_resp, response)


def solution(mesh):
    in_specs = (
        P(("wide", "narrow"), None, None),
        P(("wide", "narrow"), None, None),
        P(("wide", "narrow"), None, None),
        P(("wide", "narrow"), None, None),
        P(("wide", "narrow"), None),
        P(("wide", "narrow"), None),
        P(("wide", "narrow"), None),
        P(),
        P(None, "narrow"),
    )
    out_specs = (
        P(("wide", "narrow"), None, None),
        P(("wide", "narrow"), None, None),
        P("wide", "narrow"),
    )
    return jax.shard_map(
        per_device, mesh=mesh, in_specs=in_specs, out_specs=out_specs, check_vma=False
    )
```

```python
import functools

import jax
import jax.numpy as jnp
from jax import lax
from jax.experimental import pallas as pl
from jax.experimental.pallas import tpu as pltpu
from jax.sharding import PartitionSpec as P

BF16 = jnp.bfloat16
F32 = jnp.float32
SMEM = pl.BlockSpec(memory_space=pltpu.SMEM)
VMEM = pl.BlockSpec(memory_space=pltpu.VMEM)
ANY = pl.BlockSpec(memory_space=pl.ANY)
HBM = pl.BlockSpec(memory_space=pltpu.HBM)


def swap(value, wide_mask, narrow_mask, among=None):
    wide, narrow = lax.axis_size("wide"), lax.axis_size("narrow")
    pairs = [
        (i * narrow + j, (i ^ wide_mask) * narrow + (j ^ narrow_mask))
        for i in (among or range(wide))
        for j in range(narrow)
    ]
    return lax.ppermute(value, ("wide", "narrow"), pairs)


def call(kernel, out_shape, specs, micros, *args, scratch=(), out_specs=None, limit=32):
    return pl.pallas_call(
        kernel,
        out_shape=out_shape,
        in_specs=specs,
        out_specs=out_specs or jax.tree.map(lambda _: VMEM, out_shape),
        scratch_shapes=scratch,
        cost_estimate=pl.CostEstimate(flops=int(micros * 1e9), bytes_accessed=0, transcendentals=0),
        compiler_params=pltpu.CompilerParams(vmem_limit_bytes=limit * 1024 * 1024),
    )(*args)


def join_kernel(amps_ref, resp_ref, out_ref, sems):
    npno = amps_ref.shape[1]
    copies = []
    for i, ref in enumerate((amps_ref, resp_ref)):
        copy = pltpu.make_async_copy(ref, out_ref.at[:, :, pl.ds(i * npno, npno)], sems.at[i])
        copy.start()
        copies.append(copy)
    for copy in copies:
        copy.wait()


def pack_kernel(blk, readers_ref, couple_ref, q_ref, out_ref):
    pairs, nfun, npno = q_ref.shape
    count = (out_ref.shape[1] - nfun) // 2
    row = lax.broadcasted_iota(jnp.int32, (count, npno), 0)
    for p in range(pairs):
        for a in range(nfun // blk):
            rows = slice(a * blk, (a + 1) * blk)
            out_ref[p, rows, :] = q_ref[p, rows, :].T
        c = jnp.zeros((count, npno), F32)
        for r in range(readers_ref.shape[1]):
            c = c + jnp.where(row == readers_ref[p, r], couple_ref[p, r], 0.0)
        high = c.astype(BF16)
        out_ref[p, nfun : nfun + count, :] = high
        out_ref[p, nfun + count :, :] = (c - high.astype(F32)).astype(BF16)


def beside_kernel(places, *refs):
    *in_refs, _, out_ref = refs
    count = in_refs[0].shape[0]
    for i, ref in zip(places, in_refs):
        out_ref[i * count : (i + 1) * count] = ref[...]


def mark_kernel(*refs):
    refs[-1][...] = jnp.zeros_like(refs[-1])


def again_kernel(value_ref, after_ref, out_ref):
    del after_ref
    out_ref[...] = value_ref[...]


def load_coefficients(pack_ref, c_ref):
    count = c_ref.shape[1]
    nfun = pack_ref.shape[1] - 2 * count
    for p in range(pack_ref.shape[0]):
        c_ref[p] = pack_ref[p, nfun : nfun + count, :].astype(F32) + pack_ref[p, nfun + count :, :].astype(F32)


def add_terms(sums, overlaps, tz_ref, c_ref, dev):
    pairs, npno, _ = tz_ref.shape
    half = []
    for p, s in enumerate(overlaps):
        h = jnp.dot(s, tz_ref[p], preferred_element_type=F32)
        scaled = []
        for g in range(pairs):
            c = c_ref[g, pl.ds(dev * pairs + p, 1), :]
            c = jnp.concatenate([c, c], axis=1)
            scaled.append((h[g * npno : (g + 1) * npno] * c).astype(BF16))
        half.append(scaled)
    for g in range(pairs):
        rows = slice(g * npno, (g + 1) * npno)
        right = jnp.concatenate([s[rows] for s in overlaps], axis=1)
        left = jnp.concatenate(
            [jnp.concatenate([h[g][:, i * npno : (i + 1) * npno] for h in half], axis=1) for i in range(2)], axis=0
        )
        term = lax.dot_general(right, left, (((1,), (1,)), ((), ())), preferred_element_type=F32)
        sums[g] = term if sums[g] is None else sums[g] + term


def couple_kernel(masks, blk, narrow, flip, prior, *refs):
    where_ref, dom_ref, pack_ref = refs[:3]
    refs = refs[3:]
    q_refs, refs = refs[: len(masks)], refs[len(masks) :]
    tz_refs, refs = refs[: len(masks)], refs[len(masks) :]
    prior_ref, refs = (refs[0], refs[1:]) if prior else (None, refs)
    out_ref, spread_ref, c_ref = refs[0], refs[-2], refs[-1]
    pairs, _, npno = q_refs[0].shape
    dom_blk = q_refs[0].shape[1] // blk
    load_coefficients(pack_ref, c_ref)
    spread_ref[...] = jnp.zeros_like(spread_ref)
    for p in range(pairs):
        pair = ((where_ref[0] ^ flip) * narrow + where_ref[1]) * pairs + p
        for a in range(dom_blk):
            spread_ref[dom_ref[pair * dom_blk + a], p * npno : (p + 1) * npno, :] = pack_ref[
                p, a * blk : (a + 1) * blk, :
            ]
    sums = [None] * pairs
    for k, mask in enumerate(masks):
        dev = where_ref[0] ^ mask
        overlaps = []
        for p in range(pairs):
            pair = (dev * narrow + where_ref[1]) * pairs + p
            left = jnp.concatenate([spread_ref[dom_ref[pair * dom_blk + b]] for b in range(dom_blk)], axis=1)
            overlaps.append(jnp.dot(left, q_refs[k][p], preferred_element_type=F32).astype(BF16))
        add_terms(sums, overlaps, tz_refs[k], c_ref, dev)
    for g in range(pairs):
        for rows in (slice(0, npno), slice(npno, 2 * npno)):
            total = sums[g][:, rows].T
            out_ref[g, rows, :] = (total + prior_ref[g, rows, :] if prior else total).astype(out_ref.dtype)


def updated(p, own_ref, back_ref, amps_ref, resp_ref, ints_ref, energy_ref):
    npno = amps_ref.shape[1]
    across = jnp.broadcast_to(energy_ref[pl.ds(p, 1), :], (npno, npno))
    denom = across + across.T
    amps = amps_ref[p].astype(F32)
    resp = resp_ref[p].astype(F32)
    coupled_t = own_ref[p, :npno] + back_ref[p, :npno].astype(F32)
    coupled_z = own_ref[p, npno:] + back_ref[p, npno:].astype(F32)
    new_amps = amps - 0.5 * (ints_ref[p].astype(F32) + denom * amps + coupled_t) / denom
    new_resp = resp - 0.5 * (amps + denom * resp + coupled_z) / denom
    return new_amps, new_resp


def weights_kernel(*refs):
    w_ref = refs[-1]
    npno = w_ref.shape[2]
    row = lax.broadcasted_iota(jnp.int32, (npno, npno), 0)
    col = lax.broadcasted_iota(jnp.int32, (npno, npno), 1)
    for at in range(w_ref.shape[0]):
        both = []
        for p in (2 * at, 2 * at + 1):
            new_amps, new_resp = updated(p, *refs[:6])
            prod = lax.dot_general(
                new_amps.astype(BF16), new_resp.astype(BF16), (((1,), (1,)), ((), ())), preferred_element_type=F32
            )
            both.append(0.5 * (prod + prod.T))
        w_ref[at, :npno, :] = jnp.where(row <= col, both[0], both[1]).astype(BF16)
        diagonal = jnp.sum(jnp.where(row == col, both[1], 0.0), axis=0, keepdims=True)
        w_ref[at, npno:, :] = jnp.broadcast_to(diagonal, (w_ref.shape[1] - npno, npno)).astype(BF16)


def update_kernel(*refs):
    new_amps_ref, new_resp_ref, done_ref = refs[-3:]
    for p in range(new_amps_ref.shape[0]):
        new_amps_ref[p], new_resp_ref[p] = updated(p, *refs[:6])
    done_ref[...] = jnp.zeros_like(done_ref)


def place_kernel(blk, narrow, pairs, *refs):
    where_ref, dom_ref, ints_ref = refs[:3]
    q_refs, (full_ref, moved_ref) = refs[3 : 3 + narrow], refs[4 + narrow :]
    both, nfun, npno = q_refs[0].shape
    dom_blk = nfun // blk
    trash, rows = full_ref.shape[0] - 1, full_ref.shape[1]
    full_ref[...] = jnp.zeros_like(full_ref)
    for k in range(narrow):
        for i in range(both):
            pair = ((where_ref[0] ^ (i // pairs)) * narrow + (where_ref[1] ^ k)) * pairs + i % pairs
            slot = k * both + i
            blocks = []
            for a in range(dom_blk):
                f = dom_ref[pair * dom_blk + a]
                for j in range(blk // rows):
                    dev = f * (blk // rows) + j
                    apart = dev ^ where_ref[0]
                    at = jnp.where(apart & 1, trash, apart // 2)
                    start = a * blk + j * rows
                    full_ref[at, :, slot * npno : (slot + 1) * npno] = q_refs[k][i, start : start + rows, :]
                blocks.append(ints_ref[f])
            moved_ref[slot] = lax.dot_general(
                q_refs[k][i], jnp.concatenate(blocks, axis=0), (((0,), (0,)), ((), ())), preferred_element_type=F32
            ).astype(BF16)


def unpacked(ref, at):
    npno = ref.shape[2]
    row = lax.broadcasted_iota(jnp.int32, (npno, npno), 0)
    col = lax.broadcasted_iota(jnp.int32, (npno, npno), 1)
    mixed = ref[at, :npno, :]
    upper, lower = mixed.astype(F32), mixed.T.astype(F32)
    diagonal = jnp.broadcast_to(ref[at, npno:, :].astype(F32)[:1], (npno, npno))
    first = jnp.where(row <= col, upper, lower)
    second = jnp.where(row == col, diagonal, jnp.where(row > col, upper, lower))
    return first.astype(BF16), second.astype(BF16)


def half_response(narrow, odd, full_ref, moved_ref, w_ref, total):
    both, npno = moved_ref.shape[0] // narrow, moved_ref.shape[1]
    devs, rows = full_ref.shape[0] - 1, full_ref.shape[1]
    for k in range(odd, narrow, 2):
        parts = []
        for at in range(k // 2 * both // 2, (k // 2 + 1) * both // 2):
            for w in unpacked(w_ref, at):
                moved = moved_ref[k * both + len(parts)]
                parts.append(jnp.dot(w, moved, preferred_element_type=F32).astype(BF16))
        left = full_ref[:devs, :, k * both * npno : (k + 1) * both * npno].reshape(devs * rows, both * npno)
        term = jnp.dot(left, jnp.concatenate(parts, axis=0), preferred_element_type=F32)
        total = term if total is None else total + term
    return total


def near_kernel(narrow, full_ref, moved_ref, w_ref, out_ref):
    out_ref[...] = half_response(narrow, 0, full_ref, moved_ref, w_ref, None).reshape(out_ref.shape)


def response_kernel(others, narrow, *refs):
    full_ref, moved_ref, near_ref, w_ref = refs[:4]
    devs, rows, cols = near_ref.shape
    total = half_response(narrow, 1, full_ref, moved_ref, w_ref, near_ref[...].reshape(devs * rows, cols))
    for mask, out_ref in zip([0] + others, refs[4:]):
        out_ref[...] = total[mask // 2 * rows : (mask // 2 + 1) * rows].astype(out_ref.dtype)


def sum_kernel(*refs):
    *in_refs, _, out_ref = refs
    out_ref[...] = sum(ref[...].astype(F32) for ref in in_refs)


def per_device(amps, resp, trans, ints, energies, couple, readers, domains, integrals):
    wide, narrow = lax.axis_size("wide"), lax.axis_size("narrow")
    pairs, nfun, npno = trans.shape
    blk = nfun // domains.shape[1]
    nbas, cols = integrals.shape
    near = wide // 2
    partner = wide - 2
    sds = jax.ShapeDtypeStruct

    count = wide * pairs
    where = jnp.stack([lax.axis_index("wide"), lax.axis_index("narrow")]).astype(jnp.int32)
    dom = domains.reshape(-1)

    near_q, near_tz = {0: trans}, {}
    near_q[1] = swap(trans, 1, 0)
    for mask in range(2, near, 2):
        near_q[mask] = swap(trans, mask, 0)
    near_tz[0] = call(
        join_kernel, sds((pairs, npno, 2 * npno), BF16), [ANY, ANY], 1, amps, resp, scratch=[pltpu.SemaphoreType.DMA((2,))], limit=60,
    )
    near_tz[1] = swap(near_tz[0], 1, 0)
    for mask in range(2, near, 2):
        near_tz[mask] = swap(near_tz[0], mask, 0)
    pack = call(
        functools.partial(pack_kernel, blk),
        sds((pairs, nfun + 2 * count, npno), BF16),
        [SMEM] * 2 + [VMEM], 1,
        readers, couple, trans,
    )
    pack = call(again_kernel, sds(pack.shape, BF16), [VMEM, ANY], 0.3, pack, near_q[near - 2])
    far_pack = swap(pack, partner, 0)
    for mask in range(2, near, 2):
        near_q[mask + 1] = swap(near_q[mask], 1, 0)
        near_tz[mask + 1] = swap(near_tz[mask], 1, 0)
    early = [0, 1] + list(range(2, near, 2))
    late = list(range(3, near, 2))
    scratch = [
        pltpu.VMEM((nbas // blk, pairs * npno, blk), BF16),
        pltpu.VMEM((pairs, count, npno), F32),
    ]
    sums = sds((pairs, 2 * npno, npno), F32)
    own = call(
        functools.partial(couple_kernel, early, blk, narrow, 0, False),
        sums,
        [SMEM] * 2 + [VMEM] * (1 + 2 * len(early)), 2,
        where, dom, pack, *[near_q[m] for m in early], *[near_tz[m] for m in early],
        scratch=scratch,
    )
    far = call(
        functools.partial(couple_kernel, early + late, blk, narrow, partner, False),
        sds(sums.shape, BF16),
        [SMEM] * 2 + [VMEM] * (1 + 2 * near), 4,
        where, dom, far_pack, *[near_q[m] for m in early + late], *[near_tz[m] for m in early + late],
        scratch=scratch,
    )
    back = swap(far, partner, 0)
    own_late = call(
        functools.partial(couple_kernel, late, blk, narrow, 0, True),
        sums,
        [SMEM] * 2 + [VMEM] * (2 + 2 * len(late)), 2,
        where, dom, pack, *[near_q[m] for m in late], *[near_tz[m] for m in late], own,
        scratch=scratch,
    )
    both_q = call(
        functools.partial(beside_kernel, range(2)), sds((2 * pairs, nfun, npno), BF16), [VMEM] * 2 + [ANY], 0.3, trans, near_q[1], near_tz[1]
    )
    core_q = swap(both_q, 0, 1)
    mats = sds((pairs, npno, npno), F32)
    state = (own_late, back, amps, resp, ints, energies)
    weights = call(weights_kernel, sds((pairs // 2, npno + 16, npno), BF16), [VMEM] * 6 + [ANY], 1, *state, core_q)
    token = sds((8, 128), F32)
    new_amps, new_resp, done = call(update_kernel, (mats, mats, token), [VMEM] * 6 + [ANY], 1, *state, weights)
    narrow_q = {0: both_q, 1: core_q}
    for mask in range(2, narrow, 2):
        arrived = swap(both_q, 0, mask)
        narrow_q[mask] = call(again_kernel, sds(both_q.shape, BF16), [VMEM, ANY], 0.3, arrived, weights)
        narrow_q[mask + 1] = swap(narrow_q[mask], 0, 1)
    slots = 2 * narrow * pairs
    full, moved = call(
        functools.partial(place_kernel, blk, narrow, pairs),
        (sds((near + 1, nbas // wide, slots * npno), BF16), sds((slots, npno, cols), BF16)),
        [SMEM, SMEM] + [VMEM] * (1 + narrow) + [ANY], 1,
        where, dom, integrals.reshape(nbas // blk, blk, cols), *[narrow_q[k] for k in range(narrow)], weights,
    )
    group = [(bit, mask) for mask in range(0, narrow, 2) for bit in range(2)]
    arrived = [swap(weights, *key) if any(key) else weights for key in reversed(group)]
    near_w = call(
        functools.partial(beside_kernel, range(len(group) - 1, -1, -1)),
        sds((len(group) * pairs // 2, npno + 16, npno), BF16),
        [VMEM] * len(group) + [ANY], 0.3,
        *arrived, moved,
    )
    core_w = swap(near_w, 0, 1)
    near_part = call(
        functools.partial(near_kernel, narrow), sds((near, nbas // wide, cols), F32), [VMEM] * 3, 0.5,
        full, moved, near_w,
    )
    others = list(range(wide - 2, 0, -2))
    block = (nbas // wide, cols)
    shares = call(
        functools.partial(response_kernel, others, narrow),
        (sds(block, F32),) + (sds(block, BF16),) * len(others),
        [VMEM] * 4, 1,
        full, moved, near_part, core_w,
    )
    received = [swap(share, mask, 0) for mask, share in zip(others, shares[1:])]
    mark = call(mark_kernel, token, [ANY] * 2, 0.1, received[0], done)
    response = call(
        sum_kernel, sds(block, F32), [VMEM] * (1 + len(others)) + [ANY], 0.1, shares[0], *received, mark
    )
    return (new_amps, new_resp, response)


def solution(mesh):
    in_specs = (
        P(("wide", "narrow"), None, None),
        P(("wide", "narrow"), None, None),
        P(("wide", "narrow"), None, None),
        P(("wide", "narrow"), None, None),
        P(("wide", "narrow"), None),
        P(("wide", "narrow"), None),
        P(("wide", "narrow"), None),
        P(),
        P(None, "narrow"),
    )
    out_specs = (
        P(("wide", "narrow"), None, None),
        P(("wide", "narrow"), None, None),
        P("wide", "narrow"),
    )
    return jax.shard_map(
        per_device, mesh=mesh, in_specs=in_specs, out_specs=out_specs, check_vma=False
    )
```
